256 devices in a mesh: ctx: 128 (over x, y_hi, z, core), section: 2 (over y_lo).
Axes of the slice: x: 4, y: 4 (y_hi: 2, y_lo: 2; y = y_hi * 2 + y_lo), z: 8, core: 2. Of those that a mesh axis runs over, the one named last changes fastest.
Arguments:
- query_rows: bfloat16 [2, 32768, 4096], P('section', 'ctx'), may hold values from -140 to 140
- key_rows: bfloat16 [2, 32768, 512], P('section', 'ctx'), may hold values from -5 to 5
- value_rows: bfloat16 [2, 32768, 512], P('section', 'ctx'), may hold values from -6 to 6
- doc_lengths: int32 [32], replicated, may hold values from 256 to 1536, as said below
- rank_plan: int32 [256], replicated, may hold values from 0 to 127, as said below
- tile_mask: int32 [256, 256], replicated, may hold values from 0 to 1, as said below
Outputs:
- handed: bfloat16 [2, 49152, 4096], P('section', 'ctx')
The draws below stay inside these ranges and needn't reach their ends.
Inputs may be any that keep to these rules, and one draw needn't show every extreme that they name: `doc_lengths`: the lengths sum to 32768; the first is 256; at least one is exactly 1536. Never falling along the blocks; rank_plan[b] // 2 == b // 4; every rank holds 1 to 3 blocks and some rank exactly 3. `tile_mask`: 1 on the diagonal; off it, an entry [i, j] is 1 only where j < i and blocks i and j hold tokens of one document.
All inputs are finite; a program needn't handle non-finite values.
Results may differ from the reference program's by a relative error of at most 0.0054.
Values may be sent and summed in bfloat16 or wider, within the bound.
A program may use at most 128 MiB of HBM per device.

```python
import jax
import jax.numpy as jnp
from jax import lax

BLOCK = 128
BLK_DEV = 2
CAP = 3
DOC_BLK = 8
MOST_BLK = 12
KV_HEADS = 4
GROUP = 8
HEAD_DIM = 128
KW = 512
NBLK = 256
TOKENS = 32768
DOCS = 32
N_CTX = 128
N_SECTION = 2


def shared_keys(key):
    base_keys = jax.random.normal(key, (N_SECTION, TOKENS, KV_HEADS * HEAD_DIM), jnp.float32)
    return jnp.clip(base_keys, -5.0, 5.0)


def shared_lengths(key):
    long_count = DOCS // 2
    base = 2 * DOC_BLK - MOST_BLK
    jitter = jax.random.randint(jax.random.fold_in(key, 11), (long_count,), 0, BLOCK)
    jitter = jnp.where(jnp.arange(long_count) == long_count - 1, 0, jitter)
    short_index = jnp.arange(long_count - 1)
    short_blocks = base + 1 - 2 * (short_index % 2)
    others = jnp.sum(jnp.where(short_index < long_count - 2, short_blocks, 0))
    total_short = base * long_count - 2
    short_blocks = jnp.where(short_index == long_count - 2, total_short - others, short_blocks)
    long_len = MOST_BLK * BLOCK - jitter
    short_len = short_blocks * BLOCK + jitter[:-1]
    middle = jnp.stack([long_len[:-1], short_len], axis=1).reshape(-1)
    leading = jnp.full((1,), 2 * BLOCK, long_len.dtype)
    result = jnp.concatenate([leading, middle, long_len[-1:]], 0)
    return result.astype(jnp.int32)


def echo_source():
    positions = jnp.arange(TOKENS, dtype=jnp.int32)
    return positions


def draw_query_rows(key, part):
    base_keys = shared_keys(key)
    lengths = shared_lengths(key)
    key = jax.random.fold_in(key, 5)
    starts = jnp.cumsum(lengths) - lengths
    positions = echo_source()
    doc = jnp.sum((positions[:, None] >= starts[None, :]).astype(jnp.int32), axis=1) - 1
    doc_start = starts[doc]
    offset = positions - doc_start
    tail = offset >= (MOST_BLK - 2) * BLOCK
    match = doc_start + offset % BLOCK
    echoed = base_keys[:, match, :].reshape(N_SECTION, TOKENS, KV_HEADS, 1, HEAD_DIM)
    result = jax.random.normal(key, (N_SECTION, TOKENS, KV_HEADS, GROUP, HEAD_DIM), jnp.float32)
    result = jnp.clip(result, -5.0, 5.0)
    result = jnp.where(tail[None, :, None, None, None], echoed, result)
    return result.reshape(N_SECTION, TOKENS, KV_HEADS * GROUP * HEAD_DIM).astype(jnp.bfloat16)


def draw_key_rows(key, part):
    base_keys = shared_keys(key)
    return base_keys.astype(jnp.bfloat16)


def draw_doc_lengths(key, part):
    return shared_lengths(key)


def draw_tile_mask(key, part):
    lengths = shared_lengths(key)
    key = jax.random.fold_in(key, 21)
    ends = jnp.cumsum(lengths)
    starts = ends - lengths
    first_tok = jnp.arange(NBLK, dtype=jnp.int32) * BLOCK
    last_tok = first_tok + BLOCK - 1
    doc_first = jnp.sum((first_tok[:, None] >= starts[None, :]).astype(jnp.int32), axis=1) - 1
    doc_last = jnp.sum((last_tok[:, None] >= starts[None, :]).astype(jnp.int32), axis=1) - 1
    row_index = jnp.arange(NBLK, dtype=jnp.int32)[:, None]
    col_index = jnp.arange(NBLK, dtype=jnp.int32)[None, :]
    share = (col_index < row_index) & (doc_last[None, :] >= doc_first[:, None])
    keeper = jax.random.randint(key, (NBLK, NBLK), 0, 4) > 0
    result = (row_index == col_index) | share & keeper
    return result.astype(jnp.int32)


def draw_rank_plan(key, part):
    key = jax.random.fold_in(key, 31)
    pair_count = NBLK // (2 * BLK_DEV)
    kinds = jax.random.randint(jax.random.fold_in(key, 1), (pair_count,), 0, 3)
    forced = jax.random.randint(jax.random.fold_in(key, 2), (), 0, pair_count)
    forced_kind = 1 + jax.random.randint(jax.random.fold_in(key, 3), (), 0, 2)
    kinds = jnp.where(jnp.arange(pair_count) == forced, forced_kind, kinds)
    first_count = BLK_DEV + (kinds == 2).astype(jnp.int32) - (kinds == 1).astype(jnp.int32)
    blocks = jnp.arange(NBLK, dtype=jnp.int32)
    pair_of = blocks // (2 * BLK_DEV)
    inside = blocks % (2 * BLK_DEV)
    result = 2 * pair_of + (inside >= first_count[pair_of]).astype(jnp.int32)
    return result.astype(jnp.int32)


def steps_of(key, dims, split, least, high):
    def one(dim, blocks):
        draws = jax.random.uniform(jax.random.fold_in(jax.random.fold_in(key, 6), dim), (blocks,), jnp.float32, least / len(split), high / len(split))
        return jnp.repeat(jnp.exp(draws), dims[dim] // blocks).reshape((-1,) + (1,) * (len(dims) - dim - 1))

    level = one(*split[0])
    for cut in split[1:]:
        level = level * one(*cut)
    return level


def noise(key, extent, width, limit, shards=(), kind=jnp.bfloat16):
    factor_of = steps_of(key, extent, shards, -0.22, 0.18) if shards else 1.0
    drawn = jax.random.normal(key, extent, jnp.float32) * width * factor_of
    return jnp.minimum(jnp.maximum(drawn, -limit), limit).astype(kind)


def setup_inputs(seed: int = 0) -> dict:
    seeds = jax.random.split(jax.random.key(seed), 7)
    query_rows = draw_query_rows(jax.random.fold_in(seeds[6], 71), 0)
    key_rows = draw_key_rows(jax.random.fold_in(seeds[6], 71), 0)
    value_rows = noise(seeds[2], (N_SECTION, TOKENS, KW), 1.0, 6.0, ((0, 2), (1, 128)))
    doc_lengths = draw_doc_lengths(jax.random.fold_in(seeds[6], 71), 0)
    rank_plan = draw_rank_plan(jax.random.fold_in(seeds[6], 71), 0)
    tile_mask = draw_tile_mask(jax.random.fold_in(seeds[6], 71), 0)
    return {"query_rows": query_rows, "key_rows": key_rows, "value_rows": value_rows, "doc_lengths": doc_lengths, "rank_plan": rank_plan, "tile_mask": tile_mask}


def doc_index(positions, lengths):
    starts = jnp.cumsum(lengths) - lengths
    inside = (positions[:, None] >= starts[None, :]).astype(jnp.int32)
    return (jnp.sum(inside, axis=1) - 1).astype(jnp.int32)


def attend_batch(queries, keys, values, lengths, tile_mask):
    reach = MOST_BLK * BLOCK
    heads_kv = keys.shape[1] // HEAD_DIM
    scale = HEAD_DIM ** -0.5
    query_all = queries.reshape(NBLK, BLOCK, heads_kv, GROUP, HEAD_DIM)
    padding = jnp.zeros((reach, keys.shape[1]), keys.dtype)
    key_pad = jnp.concatenate([padding, keys], 0).reshape(-1, heads_kv, HEAD_DIM)
    value_pad = jnp.concatenate([padding, values], 0).reshape(-1, heads_kv, HEAD_DIM)

    def one_block(inputs):
        query_tile, index = inputs
        start = index * BLOCK
        key_win = lax.dynamic_slice_in_dim(key_pad, start, reach + BLOCK, 0)
        value_win = lax.dynamic_slice_in_dim(value_pad, start, reach + BLOCK, 0)
        key_pos = (start - reach + jnp.arange(reach + BLOCK, dtype=jnp.int32)).astype(jnp.int32)
        query_pos = (start + jnp.arange(BLOCK, dtype=jnp.int32)).astype(jnp.int32)
        key_block = ((key_pos + reach) // BLOCK - MOST_BLK).astype(jnp.int32)
        tiles = tile_mask[index, jnp.clip(key_block, 0, NBLK - 1)]
        same_doc = doc_index(query_pos, lengths)[:, None] == doc_index(key_pos, lengths)[None, :]
        allowed = (tiles[None, :] > 0) & (key_block[None, :] >= 0) & same_doc & (key_pos[None, :] <= query_pos[:, None])
        scores = jnp.einsum("qgho,kgo->ghqk", query_tile.astype(jnp.float32), key_win.astype(jnp.float32)) * scale
        top = jnp.max(jnp.where(allowed, scores, -1e30), axis=-1, keepdims=True)
        weights = jnp.where(allowed, jnp.exp(scores - top), 0.0)
        total = jnp.sum(weights, axis=-1)
        rounded = lax.optimization_barrier(weights.astype(jnp.bfloat16)).astype(jnp.float32)
        mixed = jnp.einsum("ghqk,kgo->qgho", rounded, value_win.astype(jnp.float32))
        result = mixed / jnp.transpose(total, (2, 0, 1))[..., None]
        return result.astype(jnp.bfloat16).reshape(BLOCK, -1)

    return lax.map(one_block, (query_all, jnp.arange(NBLK, dtype=jnp.int32)))


def reference(query_rows, key_rows, value_rows, doc_lengths, rank_plan, tile_mask):
    ranks = jnp.arange(N_CTX, dtype=jnp.int32)
    owner = (rank_plan[None, :] == ranks[:, None]).astype(jnp.int32)
    counts = jnp.sum(owner, axis=1)
    before = jnp.cumsum(counts) - counts
    slot_index = jnp.arange(CAP, dtype=jnp.int32)
    source = jnp.clip(before[:, None] + slot_index[None, :], 0, NBLK - 1).astype(jnp.int32)
    slot_valid = slot_index[None, :] < counts[:, None]
    outputs = []
    for section_index in range(N_SECTION):
        blocks = attend_batch(query_rows[section_index], key_rows[section_index], value_rows[section_index], doc_lengths, tile_mask)
        placed = jnp.where(slot_valid[:, :, None, None], blocks[source], jnp.zeros((), blocks.dtype))
        outputs.append(placed.reshape(N_CTX * CAP * BLOCK, -1))
    stacked = jnp.stack(outputs, 0)
    return jnp.roll(stacked, 1, axis=0)
```

```python
import math

import jax
import jax.numpy as jnp
from jax import lax
from jax.experimental import pallas as pl
from jax.experimental.pallas import tpu as pltpu
from jax.sharding import PartitionSpec as P

BLOCK = 128
ROWS = 256
HEADS_KV = 4
GROUP = 8
DIM = 128
WIDTH = HEADS_KV * GROUP * DIM
HEAD_COLS = GROUP * DIM
RING = 8
BAND = 13 * BLOCK
SLOTS = 11
SEG = 4
SEG_COLS = HEAD_COLS // SEG
SWAP = HEADS_KV - 1
STEPS = HEADS_KV * SEG
SENT = SWAP * SEG
FACTOR = DIM**-0.5 * math.log2(math.e)
NEG = -1e30


def attention_kernel(
    q_hbm, k_hbm, v_hbm, lengths, mask_hbm,
    recv_out, side_out,
    qbuf, kv, outb, bias, marks,
    q_sem, k_sem, v_sem, mark_sem,
    swap_send, swap_recv,
    chain_send, chain_recv,
    hop_send, hop_recv,
    sib_send, sib_recv,
    out_send, out_recv,
    mid_send, mid_recv, keep_sem,
):
    me = lax.axis_index("ctx")
    section = lax.axis_index("section")
    core = lax.rem(me, 2)
    chip = me // 2
    z = lax.rem(chip, RING)
    ring = chip // RING
    rings = lax.axis_size("ctx") // (2 * RING)

    def device(ring_at, z_at, core_at):
        return {"ctx": (ring_at * RING + z_at) * 2 + core_at, "section": section}

    z_next = lax.rem(z + 1, RING)
    z_prev = lax.rem(z + RING - 1, RING)
    sibling = device(ring, z, 1 - core)
    ahead = device(ring, z_next, core)
    behind = device(ring, z_prev, core)
    over = device(lax.rem(ring + 1, rings), z, core)
    under = device(lax.rem(ring + rings - 1, rings), z, core)
    partner = {"ctx": me, "section": 1 - section}

    def slot_of(d, z_at):
        direct = (z_at + RING - d) // RING
        return 7 + d + direct * (2 * (3 - d) + core - 7 - d)

    def remote(src, dst, send, recv, to):
        return pltpu.make_async_remote_copy(
            src_ref=src, dst_ref=dst, send_sem=send, recv_sem=recv,
            device_id=to, device_id_type=pl.DeviceIdType.MESH,
        )

    def load_q(h):
        cols = pl.ds(pl.multiple_of(h * HEAD_COLS, HEAD_COLS), HEAD_COLS)
        return pltpu.make_async_copy(q_hbm.at[:, cols], qbuf.at[h], q_sem.at[h])

    def load_kv(h):
        cols = pl.ds(pl.multiple_of(h * DIM, DIM), DIM)
        return (
            pltpu.make_async_copy(k_hbm.at[:, cols], kv.at[h, 6 + core, 0], k_sem.at[h]),
            pltpu.make_async_copy(v_hbm.at[:, cols], kv.at[h, 6 + core, 1], v_sem.at[h]),
        )

    mark_row = chip * 4 // 8 * 8
    load_marks = pltpu.make_async_copy(
        mask_hbm.at[pl.ds(pl.multiple_of(mark_row, 8), 8)], marks, mark_sem
    )

    def swap_q():
        cols = pl.ds(SWAP * HEAD_COLS, HEAD_COLS)
        return remote(q_hbm.at[:, cols], qbuf.at[SWAP], swap_send.at[2], swap_recv.at[2], partner)

    def swap_kv():
        cols = pl.ds(SWAP * DIM, DIM)
        return (
            remote(k_hbm.at[:, cols], kv.at[SWAP, 6 + core, 0],
                   swap_send.at[0], swap_recv.at[0], partner),
            remote(v_hbm.at[:, cols], kv.at[SWAP, 6 + core, 1],
                   swap_send.at[1], swap_recv.at[1], partner),
        )

    def chain(h, d, z_at=z_next):
        return remote(
            kv.at[h, slot_of(d - 1, z)], kv.at[h, slot_of(d, z_at)],
            chain_send.at[h, d - 1], chain_recv.at[h, d - 1], ahead,
        )

    def chain_wait(h, d):
        chain(h, d, z).wait_recv()

    def cross(h):
        return remote(kv.at[h, 10], kv.at[h, core],
                      hop_send.at[h, 0], hop_recv.at[h, 0], over)

    def back_a(h):
        return remote(kv.at[h, core], kv.at[h, 2 + core],
                      hop_send.at[h, 1], hop_recv.at[h, 1], behind)

    def back_b(h):
        return remote(kv.at[h, 2 + core], kv.at[h, 4 + core],
                      hop_send.at[h, 2], hop_recv.at[h, 2], behind)

    def sib(h, d, core_at=core):
        return remote(kv.at[h, (3 - d) * 2 + core], kv.at[h, (3 - d) * 2 + core_at],
                      sib_send.at[h, d], sib_recv.at[h, d], sibling)

    def sib_wait(h, d):
        sib(h, d, 1 - core).wait_recv()

    def out(i):
        return remote(outb.at[i], recv_out.at[i], out_send.at[i], out_recv.at[i], partner)

    def keep(i):
        return pltpu.make_async_copy(outb.at[i], recv_out.at[i], keep_sem.at[i - SENT])

    middle = pl.ds(pl.multiple_of((1 - core) * BLOCK, BLOCK), BLOCK)

    def mid(i, source):
        return remote(source.at[i, middle], side_out.at[i],
                      mid_send.at[i], mid_recv.at[i], sibling)

    def own_ready(h):
        @pl.when(h < SWAP)
        def _():
            for copy in load_kv(h):
                copy.wait()

        @pl.when(h == SWAP)
        def _():
            for copy in swap_kv():
                copy.wait_recv()

    def tick(h):
        @pl.when((h + 1 >= 0) & (h + 1 < HEADS_KV))
        def _():
            chain_wait(h + 1, 3)

            @pl.when(z < 3)
            def _():
                cross(h + 1).start()

            @pl.when(z >= 3)
            def _():
                sib(h + 1, 3).start()

        @pl.when((h + 2 >= 0) & (h + 2 < HEADS_KV))
        def _():
            chain_wait(h + 2, 2)
            chain(h + 2, 3).start()

            @pl.when(z >= 2)
            def _():
                sib(h + 2, 2).start()

        @pl.when((h + 3 >= 0) & (h + 3 < HEADS_KV))
        def _():
            chain_wait(h + 3, 1)
            chain(h + 3, 2).start()

            @pl.when(z >= 1)
            def _():
                sib(h + 3, 1).start()

        @pl.when((h + 4 >= 0) & (h + 4 < HEADS_KV))
        def _():
            own_ready(h + 4)
            chain(h + 4, 1).start()
            sib(h + 4, 0).start()

    def after_cross(n):
        @pl.when(z < 3)
        def _():
            cross(n).wait_recv()
            sib(n, 3).start()

            @pl.when(z >= 1)
            def _():
                back_a(n).start()

    def after_back_a(n):
        @pl.when(z < 2)
        def _():
            back_a(n).wait_recv()
            sib(n, 2).start()

            @pl.when(z == 1)
            def _():
                back_b(n).start()

    def finish(n):
        @pl.when(z == 0)
        def _():
            back_b(n).wait_recv()
            sib(n, 1).start()

        for d in range(4):
            sib_wait(n, d)

        @pl.when(n < SWAP)
        def _():
            load_q(n).wait()

        @pl.when(n == SWAP)
        def _():
            swap_q().wait_recv()

    for h in range(SWAP):
        for copy in load_kv(h):
            copy.start()
    load_marks.start()
    for h in range(SWAP):
        load_q(h).start()

    barrier = pltpu.get_barrier_semaphore()
    others = (sibling, ahead, behind, partner, over, under)
    for other in others:
        pl.semaphore_signal(barrier, inc=1, device_id=other, device_id_type=pl.DeviceIdType.MESH)
    pl.semaphore_wait(barrier, len(others))

    tick(jnp.int32(-4))
    for copy in swap_kv():
        copy.start()
    swap_q().start()

    load_marks.wait()
    first_query = (chip * 4 + core * 2) * BLOCK
    for blk in range(2):
        query = first_query + blk * BLOCK + lax.broadcasted_iota(jnp.int32, (BLOCK, BLOCK), 0)

        def latest(j, carried):
            begin, best = carried
            best = jnp.where(query >= begin, begin, best)
            return begin + lengths[j], best

        _, begin_of = lax.fori_loop(
            0, lengths.shape[0], latest, (jnp.int32(0), jnp.zeros((BLOCK, BLOCK), jnp.int32))
        )
        for j in range(13):
            key_block = chip * 4 + core * 2 + blk - 12 + j
            mark = marks[chip * 4 - mark_row + core * 2 + blk, jnp.maximum(key_block, 0)]
            key = key_block * BLOCK + lax.broadcasted_iota(jnp.int32, (BLOCK, BLOCK), 1)
            seen = (key <= query) & (key >= begin_of) & (mark > 0)
            bias[blk, :, j * BLOCK:(j + 1) * BLOCK] = jnp.where(seen, 0.0, NEG)

    tick(jnp.int32(-3))
    tick(jnp.int32(-2))
    tick(jnp.int32(-1))
    for n in range(HEADS_KV):
        after_cross(jnp.int32(n))
        after_back_a(jnp.int32(n))
        finish(jnp.int32(n))
        tick(jnp.int32(n))

    def attend(i, h, seg):
        for blk in range(2):
            at = pl.ds(blk * BLOCK, BLOCK)
            cols = [pl.ds(pl.multiple_of(seg * SEG_COLS + u * DIM, DIM), DIM) for u in range(2)]
            queries = jnp.concatenate([qbuf[h, at, c] for c in cols], 0)
            window = pl.ds(core, 7)
            keys = kv[h, window, 0].reshape(7 * ROWS, DIM)[blk * BLOCK:blk * BLOCK + BAND]
            values = kv[h, window, 1].reshape(7 * ROWS, DIM)[blk * BLOCK:blk * BLOCK + BAND]
            scores = lax.dot_general(
                queries, keys, (((1,), (1,)), ((), ())), preferred_element_type=jnp.float32
            )
            scores = scores.reshape(2, BLOCK, BAND) * FACTOR + bias[blk][None]
            top = jnp.max(scores, axis=-1, keepdims=True)
            weights = jnp.exp2(scores - top)
            total = jnp.sum(weights, axis=-1, keepdims=True)
            mixed = lax.dot_general(
                weights.astype(jnp.bfloat16).reshape(2 * BLOCK, BAND), values,
                (((1,), (0,)), ((), ())), preferred_element_type=jnp.float32,
            )
            mixed = (mixed.reshape(2, BLOCK, DIM) / total).astype(jnp.bfloat16)
            for u in range(2):
                outb[i, at, u * DIM:(u + 1) * DIM] = mixed[u]

    def step(i, _):
        h = i // SEG
        seg = lax.rem(i, SEG)
        attend(i, h, seg)

        @pl.when(h < SWAP)
        def _():
            out(i).start()

        @pl.when(h == SWAP)
        def _():
            keep(i).start()
            mid(i, outb).start()

        return 0

    lax.fori_loop(0, STEPS, step, 0)

    def pass_on(i, _):
        out(i).wait_recv()
        mid(i, recv_out).start()
        return 0

    lax.fori_loop(0, SENT, pass_on, 0)

    for copy in swap_kv():
        copy.wait_send()
    swap_q().wait_send()

    def drain(h, _):
        for d in range(3):
            chain(h, d + 1).wait_send()
        for d in range(4):
            sib(h, d).wait_send()

        @pl.when(z < 3)
        def _():
            cross(h).wait_send()

        @pl.when((z == 1) | (z == 2))
        def _():
            back_a(h).wait_send()

        @pl.when(z == 1)
        def _():
            back_b(h).wait_send()

        return 0

    lax.fori_loop(0, HEADS_KV, drain, 0)

    def drain_kept(i, _):
        keep(i).wait()
        mid(i, outb).wait()
        return 0

    lax.fori_loop(SENT, STEPS, drain_kept, 0)

    def drain_sent(i, _):
        out(i).wait_send()
        mid(i, recv_out).wait()
        return 0

    lax.fori_loop(0, SENT, drain_sent, 0)


def place_kernel(plan, own, side, placed, zeros, sems):
    me = lax.axis_index("ctx")
    core = lax.rem(me, 2)
    first = me // 2 * 4
    count = jnp.int32(0)
    for j in range(4):
        count += (plan[first + j] == me).astype(jnp.int32)
    zeros[...] = jnp.zeros_like(zeros)
    skip = jnp.where(core == 0, 0, 3 - count)

    def each(i, _):
        cols = pl.ds(pl.multiple_of(i * SEG_COLS, SEG_COLS), SEG_COLS)
        for j in range(3):
            to = placed.at[pl.ds(j * BLOCK, BLOCK), cols]
            at = j + skip
            own_at = jnp.where(core == 0, at, at - 1)
            is_side = at == jnp.where(core == 0, 2, 0)
            own_rows = pl.ds(pl.multiple_of(jnp.clip(own_at, 0, 1) * BLOCK, BLOCK), BLOCK)
            fill = pltpu.make_async_copy(zeros, to, sems.at[i, j])
            from_side = pltpu.make_async_copy(side.at[i], to, sems.at[i, j])
            from_own = pltpu.make_async_copy(own.at[i, own_rows], to, sems.at[i, j])
            pl.when(j >= count)(fill.start)
            pl.when((j < count) & is_side)(from_side.start)
            pl.when((j < count) & jnp.logical_not(is_side))(from_own.start)
        return 0

    lax.fori_loop(0, STEPS, each, 0)

    def finish(i, _):
        cols = pl.ds(pl.multiple_of(i * SEG_COLS, SEG_COLS), SEG_COLS)
        for j in range(3):
            to = placed.at[pl.ds(j * BLOCK, BLOCK), cols]
            pltpu.make_async_copy(zeros, to, sems.at[i, j]).wait()
        return 0

    lax.fori_loop(0, STEPS, finish, 0)


def body(query_rows, key_rows, value_rows, doc_lengths, rank_plan, tile_mask):
    dma = pltpu.SemaphoreType.DMA
    anywhere = pl.BlockSpec(memory_space=pl.ANY)
    scalars = pl.BlockSpec(memory_space=pltpu.SMEM)
    received, side = pl.pallas_call(
        attention_kernel,
        out_shape=(
            jax.ShapeDtypeStruct((STEPS, ROWS, SEG_COLS), jnp.bfloat16),
            jax.ShapeDtypeStruct((STEPS, BLOCK, SEG_COLS), jnp.bfloat16),
        ),
        in_specs=[anywhere, anywhere, anywhere, scalars, anywhere],
        out_specs=(anywhere, anywhere),
        scratch_shapes=[
            pltpu.VMEM((HEADS_KV, ROWS, HEAD_COLS), jnp.bfloat16),
            pltpu.VMEM((HEADS_KV, SLOTS, 2, ROWS, DIM), jnp.bfloat16),
            pltpu.VMEM((STEPS, ROWS, SEG_COLS), jnp.bfloat16),
            pltpu.VMEM((2, BLOCK, BAND), jnp.float32),
            pltpu.SMEM((8, tile_mask.shape[1]), jnp.int32),
            dma((SWAP,)), dma((SWAP,)), dma((SWAP,)), dma,
            dma((3,)), dma((3,)),
            dma((HEADS_KV, 3)), dma((HEADS_KV, 3)),
            dma((HEADS_KV, 3)), dma((HEADS_KV, 3)),
            dma((HEADS_KV, 4)), dma((HEADS_KV, 4)),
            dma((SENT,)), dma((SENT,)),
            dma((STEPS,)), dma((STEPS,)), dma((STEPS - SENT,)),
        ],
        compiler_params=pltpu.CompilerParams(
            collective_id=0, has_side_effects=True, vmem_limit_bytes=48 * 1024 * 1024
        ),
        name="attention",
    )(query_rows[0], key_rows[0], value_rows[0], doc_lengths, tile_mask)
    placed = pl.pallas_call(
        place_kernel,
        out_shape=jax.ShapeDtypeStruct((3 * BLOCK, WIDTH), jnp.bfloat16),
        in_specs=[scalars, anywhere, anywhere],
        out_specs=anywhere,
        scratch_shapes=[pltpu.VMEM((BLOCK, SEG_COLS), jnp.bfloat16), dma((STEPS, 3))],
        name="place",
    )(rank_plan, received, side)
    return placed[None]


def solution(mesh):
    placed = (
        P("section", "ctx", None),
        P("section", "ctx", None),
        P("section", "ctx", None),
        P(),
        P(),
        P(),
    )
    return jax.shard_map(
        body, mesh=mesh, in_specs=placed, out_specs=P("section", "ctx", None), check_vma=False
    )
```

```python
import math

import jax
import jax.numpy as jnp
from jax import lax
from jax.experimental import pallas as pl
from jax.experimental.pallas import tpu as pltpu
from jax.sharding import PartitionSpec as P

BLOCK = 128
ROWS = 256
HEADS_KV = 4
GROUP = 8
DIM = 128
WIDTH = HEADS_KV * GROUP * DIM
HEAD_COLS = GROUP * DIM
RING = 8
BAND = 13 * BLOCK
SLOTS = 11
SEG = 4
SEG_COLS = HEAD_COLS // SEG
SWAP = HEADS_KV - 1
STEPS = HEADS_KV * SEG
SENT = SWAP * SEG
FACTOR = DIM**-0.5 * math.log2(math.e)
NEG = -1e30


def attention_kernel(
    q_hbm, k_hbm, v_hbm, lengths_hbm, mask_hbm,
    recv_out, side_out,
    qbuf, kv, outb, bias, marks, lengths,
    q_sem, k_sem, v_sem, mark_sem, length_sem,
    swap_send, swap_recv,
    chain_send, chain_recv,
    hop_send, hop_recv,
    sib_send, sib_recv,
    out_send, out_recv,
    mid_send, mid_recv, keep_sem,
):
    me = lax.axis_index("ctx")
    section = lax.axis_index("section")
    core = lax.rem(me, 2)
    chip = me // 2
    z = lax.rem(chip, RING)
    ring = chip // RING
    rings = lax.axis_size("ctx") // (2 * RING)

    def device(ring_at, z_at, core_at):
        return {"ctx": (ring_at * RING + z_at) * 2 + core_at, "section": section}

    z_next = lax.rem(z + 1, RING)
    z_prev = lax.rem(z + RING - 1, RING)
    sibling = device(ring, z, 1 - core)
    ahead = device(ring, z_next, core)
    behind = device(ring, z_prev, core)
    over = device(lax.rem(ring + 1, rings), z, core)
    under = device(lax.rem(ring + rings - 1, rings), z, core)
    partner = {"ctx": me, "section": 1 - section}

    def slot_of(d, z_at):
        direct = (z_at + RING - d) // RING
        return 7 + d + direct * (2 * (3 - d) + core - 7 - d)

    def remote(src, dst, send, recv, to):
        return pltpu.make_async_remote_copy(
            src_ref=src, dst_ref=dst, send_sem=send, recv_sem=recv,
            device_id=to, device_id_type=pl.DeviceIdType.MESH,
        )

    def load_q(h):
        cols = pl.ds(pl.multiple_of(h * HEAD_COLS, HEAD_COLS), HEAD_COLS)
        return pltpu.make_async_copy(q_hbm.at[:, cols], qbuf[h], q_sem.at[h])

    def load_kv(h):
        cols = pl.ds(pl.multiple_of(h * DIM, DIM), DIM)
        return (
            pltpu.make_async_copy(k_hbm.at[:, cols], kv[h].at[6 + core, 0], k_sem.at[h]),
            pltpu.make_async_copy(v_hbm.at[:, cols], kv[h].at[6 + core, 1], v_sem.at[h]),
        )

    mark_row = chip * 4 // 8 * 8
    load_marks = pltpu.make_async_copy(
        mask_hbm.at[pl.ds(pl.multiple_of(mark_row, 8), 8)], marks, mark_sem
    )

    load_lengths = pltpu.make_async_copy(lengths_hbm, lengths, length_sem)

    def swap_q():
        cols = pl.ds(SWAP * HEAD_COLS, HEAD_COLS)
        return remote(q_hbm.at[:, cols], qbuf[SWAP], swap_send.at[2], swap_recv.at[2], partner)

    def swap_kv():
        cols = pl.ds(SWAP * DIM, DIM)
        return (
            remote(k_hbm.at[:, cols], kv[SWAP].at[6 + core, 0],
                   swap_send.at[0], swap_recv.at[0], partner),
            remote(v_hbm.at[:, cols], kv[SWAP].at[6 + core, 1],
                   swap_send.at[1], swap_recv.at[1], partner),
        )

    def chain(h, d, z_at=z_next):
        return remote(
            kv[h].at[slot_of(d - 1, z)], kv[h].at[slot_of(d, z_at)],
            chain_send.at[h, d - 1], chain_recv.at[h, d - 1], ahead,
        )

    def chain_wait(h, d):
        chain(h, d, z).wait_recv()

    def cross(h):
        return remote(kv[h].at[10], kv[h].at[core],
                      hop_send.at[h, 0], hop_recv.at[h, 0], over)

    def back_a(h):
        return remote(kv[h].at[core], kv[h].at[2 + core],
                      hop_send.at[h, 1], hop_recv.at[h, 1], behind)

    def back_b(h):
        return remote(kv[h].at[2 + core], kv[h].at[4 + core],
                      hop_send.at[h, 2], hop_recv.at[h, 2], behind)

    def sib(h, d, core_at=core):
        return remote(kv[h].at[(3 - d) * 2 + core], kv[h].at[(3 - d) * 2 + core_at],
                      sib_send.at[h, d], sib_recv.at[h, d], sibling)

    def sib_wait(h, d):
        sib(h, d, 1 - core).wait_recv()

    def out(i):
        return remote(outb.at[i], recv_out.at[i], out_send.at[i], out_recv.at[i], partner)

    def keep(i):
        return pltpu.make_async_copy(outb.at[i], recv_out.at[i], keep_sem.at[i - SENT])

    middle = pl.ds(pl.multiple_of((1 - core) * BLOCK, BLOCK), BLOCK)

    def mid(i, source):
        return remote(source.at[i, middle], side_out.at[i],
                      mid_send.at[i], mid_recv.at[i], sibling)

    def own_ready(h):
        if h < SWAP:
            for copy in load_kv(h):
                copy.wait()
        else:
            for copy in swap_kv():
                copy.wait_recv()

    def tick(h):
        if 0 <= h + 1 < HEADS_KV:
            chain_wait(h + 1, 3)

            @pl.when(z < 3)
            def _():
                cross(h + 1).start()

            @pl.when(z >= 3)
            def _():
                sib(h + 1, 3).start()

        if 0 <= h + 2 < HEADS_KV:
            chain_wait(h + 2, 2)
            chain(h + 2, 3).start()

            @pl.when(z >= 2)
            def _():
                sib(h + 2, 2).start()

        if 0 <= h + 3 < HEADS_KV:
            chain_wait(h + 3, 1)
            chain(h + 3, 2).start()

            @pl.when(z >= 1)
            def _():
                sib(h + 3, 1).start()

        if 0 <= h + 4 < HEADS_KV:
            own_ready(h + 4)
            chain(h + 4, 1).start()
            sib(h + 4, 0).start()

    def after_cross(n):
        @pl.when(z < 3)
        def _():
            cross(n).wait_recv()
            sib(n, 3).start()

            @pl.when(z >= 1)
            def _():
                back_a(n).start()

    def after_back_a(n):
        @pl.when(z < 2)
        def _():
            back_a(n).wait_recv()
            sib(n, 2).start()

            @pl.when(z == 1)
            def _():
                back_b(n).start()

    def finish(n):
        @pl.when(z == 0)
        def _():
            back_b(n).wait_recv()
            sib(n, 1).start()

        for d in range(4):
            sib_wait(n, d)

        if n < SWAP:
            load_q(n).wait()
        else:
            swap_q().wait_recv()

    for h in range(SWAP):
        for copy in load_kv(h):
            copy.start()
    load_marks.start()
    load_lengths.start()
    for h in range(SWAP):
        load_q(h).start()

    barrier = pltpu.get_barrier_semaphore()
    others = (sibling, ahead, behind, partner, over, under)
    for other in others:
        pl.semaphore_signal(barrier, inc=1, device_id=other, device_id_type=pl.DeviceIdType.MESH)
    pl.semaphore_wait(barrier, len(others))

    tick(-4)
    for copy in swap_kv():
        copy.start()
    swap_q().start()

    load_marks.wait()
    load_lengths.wait()
    first_query = (chip * 4 + core * 2) * BLOCK
    for blk in range(2):
        query = first_query + blk * BLOCK + lax.broadcasted_iota(jnp.int32, (BLOCK, BLOCK), 0)

        def latest(j, carried):
            begin, best = carried
            best = jnp.where(query >= begin, begin, best)
            return begin + lengths[j], best

        _, begin_of = lax.fori_loop(
            0, lengths.shape[0], latest, (jnp.int32(0), jnp.zeros((BLOCK, BLOCK), jnp.int32))
        )
        for j in range(13):
            key_block = chip * 4 + core * 2 + blk - 12 + j
            mark = marks[chip * 4 - mark_row + core * 2 + blk, jnp.maximum(key_block, 0)]
            key = key_block * BLOCK + lax.broadcasted_iota(jnp.int32, (BLOCK, BLOCK), 1)
            seen = (key <= query) & (key >= begin_of) & (mark > 0)
            bias[blk, :, j * BLOCK:(j + 1) * BLOCK] = jnp.where(seen, 0.0, NEG)

    tick(-3)
    tick(-2)
    tick(-1)
    after_cross(0)
    after_back_a(0)
    finish(0)

    def attend(i, h, seg):
        for blk in range(2):
            at = pl.ds(blk * BLOCK, BLOCK)
            cols = [pl.ds(pl.multiple_of(seg * SEG_COLS + u * DIM, DIM), DIM) for u in range(2)]
            queries = jnp.concatenate([qbuf[h][at, c] for c in cols], 0)
            window = pl.ds(core, 7)
            keys = kv[h][window, 0].reshape(7 * ROWS, DIM)[blk * BLOCK:blk * BLOCK + BAND]
            values = kv[h][window, 1].reshape(7 * ROWS, DIM)[blk * BLOCK:blk * BLOCK + BAND]
            scores = lax.dot_general(
                queries, keys, (((1,), (1,)), ((), ())), preferred_element_type=jnp.float32
            )
            scores = scores.reshape(2, BLOCK, BAND) * FACTOR + bias[blk][None]
            top = jnp.max(scores, axis=-1, keepdims=True)
            weights = jnp.exp2(scores - top)
            total = jnp.sum(weights, axis=-1, keepdims=True)
            mixed = lax.dot_general(
                weights.astype(jnp.bfloat16).reshape(2 * BLOCK, BAND), values,
                (((1,), (0,)), ((), ())), preferred_element_type=jnp.float32,
            )
            mixed = (mixed.reshape(2, BLOCK, DIM) / total).astype(jnp.bfloat16)
            for u in range(2):
                outb[i, at, u * DIM:(u + 1) * DIM] = mixed[u]

    for h in range(HEADS_KV):

        def step(seg, _):
            i = h * SEG + seg
            attend(i, h, seg)
            if h < SWAP:
                out(i).start()
            else:
                keep(i).start()
                mid(i, outb).start()

            if h + 1 < HEADS_KV:

                @pl.when(seg == 0)
                def _():
                    tick(h)

                @pl.when(seg == 1)
                def _():
                    after_cross(h + 1)

                @pl.when(seg == 2)
                def _():
                    after_back_a(h + 1)

                @pl.when(seg == 3)
                def _():
                    finish(h + 1)

            return 0

        lax.fori_loop(0, SEG, step, 0)

    def pass_on(i, _):
        out(i).wait_recv()
        mid(i, recv_out).start()
        return 0

    lax.fori_loop(0, SENT, pass_on, 0)

    for copy in swap_kv():
        copy.wait_send()
    swap_q().wait_send()

    for h in range(HEADS_KV):
        for d in range(3):
            chain(h, d + 1).wait_send()
        for d in range(4):
            sib(h, d).wait_send()

        @pl.when(z < 3)
        def _():
            cross(h).wait_send()

        @pl.when((z == 1) | (z == 2))
        def _():
            back_a(h).wait_send()

        @pl.when(z == 1)
        def _():
            back_b(h).wait_send()

    def drain_kept(i, _):
        keep(i).wait()
        mid(i, outb).wait()
        return 0

    lax.fori_loop(SENT, STEPS, drain_kept, 0)

    def drain_sent(i, _):
        out(i).wait_send()
        mid(i, recv_out).wait()
        return 0

    lax.fori_loop(0, SENT, drain_sent, 0)


def place_kernel(plan, own, side, placed, zeros, sems):
    me = lax.axis_index("ctx")
    core = lax.rem(me, 2)
    first = me // 2 * 4
    count = jnp.int32(0)
    for j in range(4):
        count += (plan[first + j] == me).astype(jnp.int32)
    zeros[...] = jnp.zeros_like(zeros)
    skip = jnp.where(core == 0, 0, 3 - count)

    def each(i, _):
        cols = pl.ds(pl.multiple_of(i * SEG_COLS, SEG_COLS), SEG_COLS)
        for j in range(3):
            to = placed.at[pl.ds(j * BLOCK, BLOCK), cols]
            at = j + skip
            own_at = jnp.where(core == 0, at, at - 1)
            is_side = at == jnp.where(core == 0, 2, 0)
            own_rows = pl.ds(pl.multiple_of(jnp.clip(own_at, 0, 1) * BLOCK, BLOCK), BLOCK)
            fill = pltpu.make_async_copy(zeros, to, sems.at[i, j])
            from_side = pltpu.make_async_copy(side.at[i], to, sems.at[i, j])
            from_own = pltpu.make_async_copy(own.at[i, own_rows], to, sems.at[i, j])
            pl.when(j >= count)(fill.start)
            pl.when((j < count) & is_side)(from_side.start)
            pl.when((j < count) & jnp.logical_not(is_side))(from_own.start)
        return 0

    lax.fori_loop(0, STEPS, each, 0)

    def finish(i, _):
        cols = pl.ds(pl.multiple_of(i * SEG_COLS, SEG_COLS), SEG_COLS)
        for j in range(3):
            to = placed.at[pl.ds(j * BLOCK, BLOCK), cols]
            pltpu.make_async_copy(zeros, to, sems.at[i, j]).wait()
        return 0

    lax.fori_loop(0, STEPS, finish, 0)


def body(query_rows, key_rows, value_rows, doc_lengths, rank_plan, tile_mask):
    dma = pltpu.SemaphoreType.DMA
    anywhere = pl.BlockSpec(memory_space=pl.ANY)
    held = pl.BlockSpec(memory_space=pltpu.HBM)
    scalars = pl.BlockSpec(memory_space=pltpu.SMEM)
    pinned = [
        pltpu.with_memory_space_constraint(x, pltpu.HBM)
        for x in (query_rows[0], key_rows[0], value_rows[0], doc_lengths, tile_mask)
    ]
    received, side = pl.pallas_call(
        attention_kernel,
        out_shape=(
            jax.ShapeDtypeStruct((STEPS, ROWS, SEG_COLS), jnp.bfloat16),
            jax.ShapeDtypeStruct((STEPS, BLOCK, SEG_COLS), jnp.bfloat16),
        ),
        in_specs=[held] * 5,
        out_specs=(anywhere, anywhere),
        scratch_shapes=[
            [pltpu.VMEM((ROWS, HEAD_COLS), jnp.bfloat16)] * HEADS_KV,
            [pltpu.VMEM((SLOTS, 2, ROWS, DIM), jnp.bfloat16)] * HEADS_KV,
            pltpu.VMEM((STEPS, ROWS, SEG_COLS), jnp.bfloat16),
            pltpu.VMEM((2, BLOCK, BAND), jnp.float32),
            pltpu.SMEM((8, tile_mask.shape[1]), jnp.int32),
            pltpu.SMEM(doc_lengths.shape, jnp.int32),
            dma((SWAP,)), dma((SWAP,)), dma((SWAP,)), dma, dma,
            dma((3,)), dma((3,)),
            dma((HEADS_KV, 3)), dma((HEADS_KV, 3)),
            dma((HEADS_KV, 3)), dma((HEADS_KV, 3)),
            dma((HEADS_KV, 4)), dma((HEADS_KV, 4)),
            dma((SENT,)), dma((SENT,)),
            dma((STEPS,)), dma((STEPS,)), dma((STEPS - SENT,)),
        ],
        compiler_params=pltpu.CompilerParams(
            collective_id=0, has_side_effects=True, vmem_limit_bytes=48 * 1024 * 1024
        ),
        name="attention",
    )(*pinned)
    placed = pl.pallas_call(
        place_kernel,
        out_shape=jax.ShapeDtypeStruct((3 * BLOCK, WIDTH), jnp.bfloat16),
        in_specs=[scalars, anywhere, anywhere],
        out_specs=held,
        compiler_params=pltpu.CompilerParams(vmem_limit_bytes=8 * 1024 * 1024),
        scratch_shapes=[pltpu.VMEM((BLOCK, SEG_COLS), jnp.bfloat16), dma((STEPS, 3))],
        name="place",
    )(rank_plan, received, side)
    return placed[None]


def solution(mesh):
    placed = (
        P("section", "ctx", None),
        P("section", "ctx", None),
        P("section", "ctx", None),
        P(),
        P(),
        P(),
    )
    return jax.shard_map(
        body, mesh=mesh, in_specs=placed, out_specs=P("section", "ctx", None), check_vma=False
    )
```

```python
import math

import jax
import jax.numpy as jnp
from jax import lax
from jax.experimental import pallas as pl
from jax.experimental.pallas import tpu as pltpu
from jax.sharding import PartitionSpec as P

BLOCK = 128
ROWS = 256
HEADS_KV = 4
GROUP = 8
DIM = 128
WIDTH = HEADS_KV * GROUP * DIM
HEAD_COLS = GROUP * DIM
RING = 8
BAND = 13 * BLOCK
PART = 4 * BLOCK
SLOTS = 10
SEG = 4
SEG_COLS = HEAD_COLS // SEG
SWAP = HEADS_KV - 1
STEPS = HEADS_KV * SEG
SENT = SWAP * SEG
FACTOR = DIM**-0.5 * math.log2(math.e)
NEG = -1e30


def attention_kernel(
    q_hbm, k_hbm, v_hbm, lengths_hbm, mask_hbm,
    recv_out, side_out,
    qbuf, kv, outb, bias, marks, lengths,
    q_sem, k_sem, v_sem, mark_sem, length_sem,
    swap_send, swap_recv,
    chain_send, chain_recv,
    hop_send, hop_recv, cross_send, cross_recv,
    sib_send, sib_recv,
    out_send, out_recv,
    mid_send, mid_recv, keep_sem,
):
    me = lax.axis_index("ctx")
    section = lax.axis_index("section")
    core = lax.rem(me, 2)
    chip = me // 2
    z = lax.rem(chip, RING)
    ring = chip // RING
    rings = lax.axis_size("ctx") // (2 * RING)

    def device(ring_at, z_at, core_at):
        return {"ctx": (ring_at * RING + z_at) * 2 + core_at, "section": section}

    z_next = lax.rem(z + 1, RING)
    z_prev = lax.rem(z + RING - 1, RING)
    sibling = device(ring, z, 1 - core)
    ahead = device(ring, z_next, core)
    behind = device(ring, z_prev, core)
    over = device(lax.rem(ring + 1, rings), z, core)
    under = device(lax.rem(ring + rings - 1, rings), z, core)
    partner = {"ctx": me, "section": 1 - section}

    def held(d):
        return (3 - d) * 2 + core

    def remote(src, dst, send, recv, to):
        return pltpu.make_async_remote_copy(
            src_ref=src, dst_ref=dst, send_sem=send, recv_sem=recv,
            device_id=to, device_id_type=pl.DeviceIdType.MESH,
        )

    def load_q(h):
        cols = pl.ds(pl.multiple_of(h * HEAD_COLS, HEAD_COLS), HEAD_COLS)
        return pltpu.make_async_copy(q_hbm.at[:, cols], qbuf[h], q_sem.at[h])

    def load_kv(h):
        cols = pl.ds(pl.multiple_of(h * DIM, DIM), DIM)
        return (
            pltpu.make_async_copy(k_hbm.at[:, cols], kv[h].at[6 + core, 0], k_sem.at[h]),
            pltpu.make_async_copy(v_hbm.at[:, cols], kv[h].at[6 + core, 1], v_sem.at[h]),
        )

    mark_row = chip * 4 // 8 * 8
    load_marks = pltpu.make_async_copy(
        mask_hbm.at[pl.ds(pl.multiple_of(mark_row, 8), 8)], marks, mark_sem
    )

    load_lengths = pltpu.make_async_copy(lengths_hbm, lengths, length_sem)

    def swap_q(seg):
        cols = pl.ds(SWAP * HEAD_COLS + seg * SEG_COLS, SEG_COLS)
        to = pl.ds(seg * SEG_COLS, SEG_COLS)
        return remote(q_hbm.at[:, cols], qbuf[SWAP].at[:, to],
                      swap_send.at[2 + seg], swap_recv.at[2 + seg], partner)

    def swap_kv():
        cols = pl.ds(SWAP * DIM, DIM)
        return (
            remote(k_hbm.at[:, cols], kv[SWAP].at[6 + core, 0],
                   swap_send.at[0], swap_recv.at[0], partner),
            remote(v_hbm.at[:, cols], kv[SWAP].at[6 + core, 1],
                   swap_send.at[1], swap_recv.at[1], partner),
        )

    def chain(h, d):
        return remote(kv[h].at[held(d - 1)], kv[h].at[held(d)],
                      chain_send.at[h, d - 1], chain_recv.at[h, d - 1], ahead)

    def cross(h):
        return remote(kv[h].at[6 + core], kv[h].at[8], cross_send.at[h], cross_recv.at[h], over)

    def wrap(h):
        return remote(kv[h].at[8], kv[h].at[held(1)], chain_send.at[h, 0], chain_recv.at[h, 0], ahead)

    def stride_one(h):
        return remote(kv[h].at[8], kv[h].at[9], hop_send.at[h, 0], hop_recv.at[h, 0],
                      device(ring, lax.rem(z + RING - 3, RING), core))

    def stride_two(h, d):
        return remote(kv[h].at[9], kv[h].at[held(d)], hop_send.at[h, d - 1], hop_recv.at[h, d - 1],
                      device(ring, 0, core))

    def sib(h, d, core_at=core):
        return remote(kv[h].at[(3 - d) * 2 + core], kv[h].at[(3 - d) * 2 + core_at],
                      sib_send.at[h, d], sib_recv.at[h, d], sibling)

    def sib_wait(h, d):
        sib(h, d, 1 - core).wait_recv()

    def out(i):
        return remote(outb.at[i], recv_out.at[i], out_send.at[i], out_recv.at[i], partner)

    def keep(i):
        return pltpu.make_async_copy(outb.at[i], recv_out.at[i], keep_sem.at[i - SENT])

    middle = pl.ds(pl.multiple_of((1 - core) * BLOCK, BLOCK), BLOCK)

    def mid(i, source):
        return remote(source.at[i, middle], side_out.at[i],
                      mid_send.at[i], mid_recv.at[i], sibling)

    def own_ready(h):
        if h < SWAP:
            for copy in load_kv(h):
                copy.wait()
        else:
            for copy in swap_kv():
                copy.wait_recv()

    def at_z(place, *actions):
        @pl.when(z == place)
        def _():
            for action in actions:
                action()

    def ready(n, e):
        if e < 3:

            @pl.when(z < RING - 1)
            def _():
                chain(n, e + 1).start()

        sib(n, e).start()

    def arrive(n, d):
        chain(n, d).wait_recv()
        ready(n, d)

    def arrive_over(n, d):
        if d == 1:
            chain(n, d).wait_recv()
        else:
            at_z(0, stride_two(n, d).wait_recv)
            pl.when(z > 0)(chain(n, d).wait_recv)
        ready(n, d)

    def own(n):
        own_ready(n)

        @pl.when(z >= RING - 3)
        def _():
            cross(n).start()

    def tick(h):
        now = h + 4
        for n in range(HEADS_KV):
            if now == n == 0:
                own(n)
        for d in (3, 2, 1):
            if 0 <= now - d - 1 < HEADS_KV:
                pl.when(z < d)(lambda: arrive_over(now - d - 1, d))
            if 0 <= now - d < HEADS_KV:
                pl.when(z >= d)(lambda: arrive(now - d, d))
        if now < HEADS_KV:
            ready(now, 0)
        if now + 1 < HEADS_KV:
            own(now + 1)
        for n in range(HEADS_KV):
            if now == max(2, n + 1):
                at_z(3, stride_one(n).wait_recv, stride_two(n, 2).start)
                at_z(2, stride_one(n).wait_recv, stride_two(n, 3).start)
            if now == max(1, n):
                at_z(RING - 1, cross(n).wait_recv, wrap(n).start)

                @pl.when((z == RING - 2) | (z == RING - 3))
                def _():
                    cross(n).wait_recv()
                    stride_one(n).start()

    def finish(n):
        for d in range(4):
            sib_wait(n, d)

        if n < SWAP:
            load_q(n).wait()
        else:
            for seg in range(SEG):
                swap_q(seg).wait_recv()

    for h in range(SWAP):
        for copy in load_kv(h):
            copy.start()
    load_marks.start()
    load_lengths.start()
    for h in range(SWAP):
        load_q(h).start()

    barrier = pltpu.get_barrier_semaphore()
    def greet(other):
        pl.semaphore_signal(barrier, inc=1, device_id=other, device_id_type=pl.DeviceIdType.MESH)

    for other in (sibling, ahead, behind, partner):
        greet(other)
    pairs = ((5, 2), (6, 3), (3, 0), (2, 0))
    for a, b in pairs:
        at_z(a, lambda: greet(device(ring, b, core)))
        at_z(b, lambda: greet(device(ring, a, core)))

    @pl.when(z >= RING - 3)
    def _():
        greet(over)
        greet(under)

    for place in range(RING):
        greeted = 4 + 2 * (place >= RING - 3) + sum(pair.count(place) for pair in pairs)
        at_z(place, lambda: pl.semaphore_wait(barrier, greeted))

    tick(-4)
    for copy in swap_kv():
        copy.start()
    swap_q(0).start()

    load_marks.wait()
    load_lengths.wait()
    first_query = (chip * 4 + core * 2) * BLOCK
    for blk in range(2):
        query = first_query + blk * BLOCK + lax.broadcasted_iota(jnp.int32, (BLOCK, BLOCK), 0)

        def latest(j, carried):
            begin, best = carried
            best = jnp.where(query >= begin, begin, best)
            return begin + lengths[j], best

        _, begin_of = lax.fori_loop(
            0, lengths.shape[0], latest, (jnp.int32(0), jnp.zeros((BLOCK, BLOCK), jnp.int32))
        )
        for j in range(13):
            key_block = chip * 4 + core * 2 + blk - 12 + j
            mark = marks[chip * 4 - mark_row + core * 2 + blk, jnp.maximum(key_block, 0)]
            key = key_block * BLOCK + lax.broadcasted_iota(jnp.int32, (BLOCK, BLOCK), 1)
            seen = (key <= query) & (key >= begin_of) & (mark > 0)
            bias[blk, :, j * BLOCK:(j + 1) * BLOCK] = jnp.where(seen, 0.0, NEG)

    for h in (-3, -2, -1):
        tick(h)
        swap_q(h + 4).start()

    def early_tick(h):
        pl.when(z < 3)(lambda: tick(h))

    def late_tick(h):
        pl.when(z >= 3)(lambda: tick(h))

    early_tick(0)
    finish(0)

    def attend(i, h, seg):
        for blk in range(2):
            at = pl.ds(blk * BLOCK, BLOCK)
            cols = [pl.ds(pl.multiple_of(seg * SEG_COLS + u * DIM, DIM), DIM) for u in range(2)]
            queries = jnp.concatenate([qbuf[h][at, c] for c in cols], 0)
            window = pl.ds(core, 7)
            keys = kv[h][window, 0].reshape(7 * ROWS, DIM)[blk * BLOCK:blk * BLOCK + BAND]
            values = kv[h][window, 1].reshape(7 * ROWS, DIM)[blk * BLOCK:blk * BLOCK + BAND]
            parts = []
            top = None
            for first in range(0, BAND, PART):
                cut = slice(first, min(first + PART, BAND))
                scores = lax.dot_general(
                    queries, keys[cut], (((1,), (1,)), ((), ())), preferred_element_type=jnp.float32
                )
                scores = scores.reshape(2, BLOCK, -1) * FACTOR + bias[blk, :, cut][None]
                parts.append((cut, scores))
                highest = jnp.max(scores, axis=-1, keepdims=True)
                top = highest if top is None else jnp.maximum(top, highest)
            mixed = jnp.zeros((2 * BLOCK, 2 * DIM), jnp.float32)
            for cut, scores in parts:
                weights = jnp.exp2(scores - top).astype(jnp.bfloat16).reshape(2 * BLOCK, -1)
                summed = jnp.concatenate([values[cut], jnp.ones_like(values[cut])], 1)
                mixed += lax.dot_general(
                    weights, summed, (((1,), (0,)), ((), ())), preferred_element_type=jnp.float32
                )
            mixed = (mixed[:, :DIM] / mixed[:, DIM:]).astype(jnp.bfloat16).reshape(2, BLOCK, DIM)
            for u in range(2):
                outb[i, at, u * DIM:(u + 1) * DIM] = mixed[u]

    services = (
        ((), (lambda: late_tick(0),), (), (lambda: early_tick(1), lambda: finish(1))),
        ((lambda: late_tick(1),), (), (), (lambda: early_tick(2), lambda: finish(2))),
        ((lambda: late_tick(2),), (), (), (lambda: early_tick(3), lambda: finish(3))),
        ((), (), (), ()),
    )

    for h in range(HEADS_KV):

        def step(seg, _):
            i = h * SEG + seg
            attend(i, h, seg)
            if h < SWAP:
                out(i).start()
            else:
                keep(i).start()
                mid(i, outb).start()

            for at in range(SEG):
                if services[h][at]:

                    @pl.when(seg == at)
                    def _():
                        for service in services[h][at]:
                            service()

            return 0

        lax.fori_loop(0, SEG, step, 0)

    def pass_on(i, _):
        out(i).wait_recv()
        mid(i, recv_out).start()
        return 0

    lax.fori_loop(0, SENT, pass_on, 0)

    for copy in swap_kv():
        copy.wait_send()
    for seg in range(SEG):
        swap_q(seg).wait_send()

    for h in range(HEADS_KV):
        for d in (1, 2, 3):
            pl.when(z < RING - 1)(chain(h, d).wait_send)
        pl.when(z >= RING - 3)(cross(h).wait_send)
        at_z(RING - 1, wrap(h).wait_send)
        pl.when((z == RING - 2) | (z == RING - 3))(stride_one(h).wait_send)
        at_z(3, stride_two(h, 2).wait_send)
        at_z(2, stride_two(h, 3).wait_send)
        for d in range(4):
            sib(h, d).wait_send()

    def drain_kept(i, _):
        keep(i).wait()
        mid(i, outb).wait()
        return 0

    lax.fori_loop(SENT, STEPS, drain_kept, 0)

    def drain_sent(i, _):
        out(i).wait_send()
        mid(i, recv_out).wait()
        return 0

    lax.fori_loop(0, SENT, drain_sent, 0)


def place_kernel(plan, own, side, placed, zeros, sems):
    me = lax.axis_index("ctx")
    core = lax.rem(me, 2)
    first = me // 2 * 4
    count = jnp.int32(0)
    for j in range(4):
        count += (plan[first + j] == me).astype(jnp.int32)
    zeros[...] = jnp.zeros_like(zeros)
    skip = jnp.where(core == 0, 0, 3 - count)

    def each(i, _):
        cols = pl.ds(pl.multiple_of(i * SEG_COLS, SEG_COLS), SEG_COLS)
        for j in range(3):
            to = placed.at[pl.ds(j * BLOCK, BLOCK), cols]
            at = j + skip
            own_at = jnp.where(core == 0, at, at - 1)
            is_side = at == jnp.where(core == 0, 2, 0)
            own_rows = pl.ds(pl.multiple_of(jnp.clip(own_at, 0, 1) * BLOCK, BLOCK), BLOCK)
            fill = pltpu.make_async_copy(zeros, to, sems.at[i, j])
            from_side = pltpu.make_async_copy(side.at[i], to, sems.at[i, j])
            from_own = pltpu.make_async_copy(own.at[i, own_rows], to, sems.at[i, j])
            pl.when(j >= count)(fill.start)
            pl.when((j < count) & is_side)(from_side.start)
            pl.when((j < count) & jnp.logical_not(is_side))(from_own.start)
        return 0

    lax.fori_loop(0, STEPS, each, 0)

    def finish(i, _):
        cols = pl.ds(pl.multiple_of(i * SEG_COLS, SEG_COLS), SEG_COLS)
        for j in range(3):
            to = placed.at[pl.ds(j * BLOCK, BLOCK), cols]
            pltpu.make_async_copy(zeros, to, sems.at[i, j]).wait()
        return 0

    lax.fori_loop(0, STEPS, finish, 0)


def body(query_rows, key_rows, value_rows, doc_lengths, rank_plan, tile_mask):
    dma = pltpu.SemaphoreType.DMA
    anywhere = pl.BlockSpec(memory_space=pl.ANY)
    held = pl.BlockSpec(memory_space=pltpu.HBM)
    scalars = pl.BlockSpec(memory_space=pltpu.SMEM)
    pinned = [
        pltpu.with_memory_space_constraint(x, pltpu.HBM)
        for x in (query_rows[0], key_rows[0], value_rows[0], doc_lengths, tile_mask)
    ]
    received, side = pl.pallas_call(
        attention_kernel,
        out_shape=(
            jax.ShapeDtypeStruct((STEPS, ROWS, SEG_COLS), jnp.bfloat16),
            jax.ShapeDtypeStruct((STEPS, BLOCK, SEG_COLS), jnp.bfloat16),
        ),
        in_specs=[held] * 5,
        out_specs=(anywhere, anywhere),
        scratch_shapes=[
            [pltpu.VMEM((ROWS, HEAD_COLS), jnp.bfloat16)] * HEADS_KV,
            [pltpu.VMEM((SLOTS, 2, ROWS, DIM), jnp.bfloat16)] * HEADS_KV,
            pltpu.VMEM((STEPS, ROWS, SEG_COLS), jnp.bfloat16),
            pltpu.VMEM((2, BLOCK, BAND), jnp.float32),
            pltpu.SMEM((8, tile_mask.shape[1]), jnp.int32),
            pltpu.SMEM(doc_lengths.shape, jnp.int32),
            dma((SWAP,)), dma((SWAP,)), dma((SWAP,)), dma, dma,
            dma((2 + SEG,)), dma((2 + SEG,)),
            dma((HEADS_KV, 3)), dma((HEADS_KV, 3)),
            dma((HEADS_KV, 3)), dma((HEADS_KV, 3)), dma((HEADS_KV,)), dma((HEADS_KV,)),
            dma((HEADS_KV, 4)), dma((HEADS_KV, 4)),
            dma((SENT,)), dma((SENT,)),
            dma((STEPS,)), dma((STEPS,)), dma((STEPS - SENT,)),
        ],
        compiler_params=pltpu.CompilerParams(
            collective_id=0, has_side_effects=True, vmem_limit_bytes=48 * 1024 * 1024
        ),
        name="attention",
    )(*pinned)
    placed = pl.pallas_call(
        place_kernel,
        out_shape=jax.ShapeDtypeStruct((3 * BLOCK, WIDTH), jnp.bfloat16),
        in_specs=[scalars, anywhere, anywhere],
        out_specs=held,
        compiler_params=pltpu.CompilerParams(vmem_limit_bytes=8 * 1024 * 1024),
        scratch_shapes=[pltpu.VMEM((BLOCK, SEG_COLS), jnp.bfloat16), dma((STEPS, 3))],
        name="place",
    )(rank_plan, received, side)
    return placed[None]


def solution(mesh):
    placed = (
        P("section", "ctx", None),
        P("section", "ctx", None),
        P("section", "ctx", None),
        P(),
        P(),
        P(),
    )
    return jax.shard_map(
        body, mesh=mesh, in_specs=placed, out_specs=P("section", "ctx", None), check_vma=False
    )
```

```python
import math

import jax
import jax.numpy as jnp
from jax import lax
from jax.experimental import pallas as pl
from jax.experimental.pallas import tpu as pltpu
from jax.sharding import PartitionSpec as P

BLOCK = 128
ROWS = 256
HEADS_KV = 4
GROUP = 8
DIM = 128
WIDTH = HEADS_KV * GROUP * DIM
HEAD_COLS = GROUP * DIM
RING = 8
BAND = 13 * BLOCK
PART = 4 * BLOCK
SLOTS = 10
SEG = 4
SEG_COLS = HEAD_COLS // SEG
SWAP = HEADS_KV - 1
STEPS = HEADS_KV * SEG
SENT = SWAP * SEG
FACTOR = DIM**-0.5 * math.log2(math.e)
NEG = -1e30


def attention_kernel(
    q_hbm, k_hbm, v_hbm, lengths_hbm, mask_hbm,
    recv_out, side_out,
    qbuf, kv, outb, bias, marks, lengths,
    q_sem, k_sem, v_sem, mark_sem, length_sem,
    swap_send, swap_recv,
    chain_send, chain_recv,
    hop_send, hop_recv, cross_send, cross_recv,
    sib_send, sib_recv,
    out_send, out_recv,
    mid_send, mid_recv, keep_sem,
):
    me = lax.axis_index("ctx")
    section = lax.axis_index("section")
    core = lax.rem(me, 2)
    chip = me // 2
    z = lax.rem(chip, RING)
    ring = chip // RING
    rings = lax.axis_size("ctx") // (2 * RING)

    def device(ring_at, z_at, core_at):
        return {"ctx": (ring_at * RING + z_at) * 2 + core_at, "section": section}

    z_next = lax.rem(z + 1, RING)
    z_prev = lax.rem(z + RING - 1, RING)
    sibling = device(ring, z, 1 - core)
    ahead = device(ring, z_next, core)
    behind = device(ring, z_prev, core)
    over = device(lax.rem(ring + 1, rings), z, core)
    under = device(lax.rem(ring + rings - 1, rings), z, core)
    partner = {"ctx": me, "section": 1 - section}

    def held(d):
        return (3 - d) * 2 + core

    def remote(src, dst, send, recv, to):
        return pltpu.make_async_remote_copy(
            src_ref=src, dst_ref=dst, send_sem=send, recv_sem=recv,
            device_id=to, device_id_type=pl.DeviceIdType.MESH,
        )

    def load_q(h):
        cols = pl.ds(pl.multiple_of(h * HEAD_COLS, HEAD_COLS), HEAD_COLS)
        return pltpu.make_async_copy(q_hbm.at[:, cols], qbuf[h], q_sem.at[h])

    def load_kv(h):
        cols = pl.ds(pl.multiple_of(h * DIM, DIM), DIM)
        return (
            pltpu.make_async_copy(k_hbm.at[:, cols], kv[h].at[6 + core, 0], k_sem.at[h]),
            pltpu.make_async_copy(v_hbm.at[:, cols], kv[h].at[6 + core, 1], v_sem.at[h]),
        )

    mark_row = chip * 4 // 8 * 8
    load_marks = pltpu.make_async_copy(
        mask_hbm.at[pl.ds(pl.multiple_of(mark_row, 8), 8)], marks, mark_sem
    )

    load_lengths = pltpu.make_async_copy(lengths_hbm, lengths, length_sem)

    def swap_q(seg):
        cols = pl.ds(SWAP * HEAD_COLS + seg * SEG_COLS, SEG_COLS)
        to = pl.ds(seg * SEG_COLS, SEG_COLS)
        return remote(q_hbm.at[:, cols], qbuf[SWAP].at[:, to],
                      swap_send.at[2 + seg], swap_recv.at[2 + seg], partner)

    def swap_kv():
        cols = pl.ds(SWAP * DIM, DIM)
        return (
            remote(k_hbm.at[:, cols], kv[SWAP].at[6 + core, 0],
                   swap_send.at[0], swap_recv.at[0], partner),
            remote(v_hbm.at[:, cols], kv[SWAP].at[6 + core, 1],
                   swap_send.at[1], swap_recv.at[1], partner),
        )

    def chain(h, d):
        return remote(kv[h].at[held(d - 1)], kv[h].at[held(d)],
                      chain_send.at[h, d - 1], chain_recv.at[h, d - 1], ahead)

    def cross(h):
        return remote(kv[h].at[6 + core], kv[h].at[8], cross_send.at[h], cross_recv.at[h], over)

    def wrap(h):
        return remote(kv[h].at[8], kv[h].at[held(1)], chain_send.at[h, 0], chain_recv.at[h, 0], ahead)

    def stride_one(h):
        return remote(kv[h].at[8], kv[h].at[9], hop_send.at[h, 0], hop_recv.at[h, 0],
                      device(ring, lax.rem(z + RING - 3, RING), core))

    def stride_two(h, d):
        return remote(kv[h].at[9], kv[h].at[held(d)], hop_send.at[h, d - 1], hop_recv.at[h, d - 1],
                      device(ring, 0, core))

    def sib(h, d, core_at=core):
        return remote(kv[h].at[(3 - d) * 2 + core], kv[h].at[(3 - d) * 2 + core_at],
                      sib_send.at[h, d], sib_recv.at[h, d], sibling)

    def sib_wait(h, d):
        sib(h, d, 1 - core).wait_recv()

    def out(i):
        return remote(outb.at[i], recv_out.at[i], out_send.at[i], out_recv.at[i], partner)

    def keep(i):
        return pltpu.make_async_copy(outb.at[i], recv_out.at[i], keep_sem.at[i - SENT])

    middle = pl.ds(pl.multiple_of((1 - core) * BLOCK, BLOCK), BLOCK)

    def mid(i, source):
        return remote(source.at[i, middle], side_out.at[i],
                      mid_send.at[i], mid_recv.at[i], sibling)

    def own_ready(h):
        if h < SWAP:
            for copy in load_kv(h):
                copy.wait()
        else:
            for copy in swap_kv():
                copy.wait_recv()

    def at_z(place, *actions):
        @pl.when(z == place)
        def _():
            for action in actions:
                action()

    def ready(n, e):
        if e < 3:

            @pl.when(z < RING - 1)
            def _():
                chain(n, e + 1).start()

        sib(n, e).start()

    def arrive(n, d):
        chain(n, d).wait_recv()
        ready(n, d)

    def arrive_over(n, d):
        if d == 1:
            chain(n, d).wait_recv()
        else:
            at_z(0, stride_two(n, d).wait_recv)
            pl.when(z > 0)(chain(n, d).wait_recv)
        ready(n, d)

    def own(n):
        own_ready(n)

        @pl.when(z >= RING - 3)
        def _():
            cross(n).start()

    def tick(h):
        now = h + 4
        for n in range(HEADS_KV):
            if now == n == 0:
                own(n)
        for d in (3, 2, 1):
            if 0 <= now - d - 1 < HEADS_KV and (now, d) != (4, 3):
                pl.when(z < d)(lambda: arrive_over(now - d - 1, d))
            if 0 <= now - d < HEADS_KV:
                pl.when(z >= d)(lambda: arrive(now - d, d))
        if now < HEADS_KV:
            ready(now, 0)
        if now + 1 < HEADS_KV:
            own(now + 1)
        for n in range(HEADS_KV):
            if now == max(2, n + 1):
                at_z(3, stride_one(n).wait_recv, stride_two(n, 2).start)
                at_z(2, stride_one(n).wait_recv, stride_two(n, 3).start)
            if now == max(1, n):
                at_z(RING - 1, cross(n).wait_recv, wrap(n).start)

                @pl.when((z == RING - 2) | (z == RING - 3))
                def _():
                    cross(n).wait_recv()
                    stride_one(n).start()

    def finish(n):
        for d in range(4):
            sib_wait(n, d)

        if n < SWAP:
            load_q(n).wait()
        else:
            for seg in range(SEG):
                swap_q(seg).wait_recv()

    for h in range(SWAP):
        for copy in load_kv(h):
            copy.start()
    load_marks.start()
    load_lengths.start()
    for h in range(SWAP):
        load_q(h).start()

    barrier = pltpu.get_barrier_semaphore()
    def greet(other):
        pl.semaphore_signal(barrier, inc=1, device_id=other, device_id_type=pl.DeviceIdType.MESH)

    for other in (sibling, ahead, behind, partner):
        greet(other)
    pairs = ((5, 2), (6, 3), (3, 0), (2, 0))
    for a, b in pairs:
        at_z(a, lambda: greet(device(ring, b, core)))
        at_z(b, lambda: greet(device(ring, a, core)))

    @pl.when(z >= RING - 3)
    def _():
        greet(over)
        greet(under)

    for place in range(RING):
        greeted = 4 + 2 * (place >= RING - 3) + sum(pair.count(place) for pair in pairs)
        at_z(place, lambda: pl.semaphore_wait(barrier, greeted))

    tick(-4)
    for copy in swap_kv():
        copy.start()
    swap_q(0).start()

    load_marks.wait()
    load_lengths.wait()
    first_query = (chip * 4 + core * 2) * BLOCK
    for blk in range(2):
        query = first_query + blk * BLOCK + lax.broadcasted_iota(jnp.int32, (BLOCK, BLOCK), 0)

        def latest(j, carried):
            begin, best = carried
            best = jnp.where(query >= begin, begin, best)
            return begin + lengths[j], best

        _, begin_of = lax.fori_loop(
            0, lengths.shape[0], latest, (jnp.int32(0), jnp.zeros((BLOCK, BLOCK), jnp.int32))
        )
        for j in range(13):
            key_block = chip * 4 + core * 2 + blk - 12 + j
            mark = marks[chip * 4 - mark_row + core * 2 + blk, jnp.maximum(key_block, 0)]
            key = key_block * BLOCK + lax.broadcasted_iota(jnp.int32, (BLOCK, BLOCK), 1)
            seen = (key <= query) & (key >= begin_of) & (mark > 0)
            bias[blk, :, j * BLOCK:(j + 1) * BLOCK] = jnp.where(seen, 0.0, NEG)

    for h in (-3, -2, -1):
        tick(h)
        swap_q(h + 4).start()

    def early_tick(h):
        pl.when(z < 3)(lambda: tick(h))

    def late_tick(h):
        pl.when(z >= 3)(lambda: tick(h))

    pl.when(z < 3)(lambda: arrive_over(0, 3))
    finish(0)

    def attend(i, h, seg):
        for blk in range(2):
            at = pl.ds(blk * BLOCK, BLOCK)
            cols = [pl.ds(pl.multiple_of(seg * SEG_COLS + u * DIM, DIM), DIM) for u in range(2)]
            queries = jnp.concatenate([qbuf[h][at, c] for c in cols], 0)
            window = pl.ds(core, 7)
            keys = kv[h][window, 0].reshape(7 * ROWS, DIM)[blk * BLOCK:blk * BLOCK + BAND]
            values = kv[h][window, 1].reshape(7 * ROWS, DIM)[blk * BLOCK:blk * BLOCK + BAND]
            parts = []
            top = None
            for first in range(0, BAND, PART):
                cut = slice(first, min(first + PART, BAND))
                scores = lax.dot_general(
                    queries, keys[cut], (((1,), (1,)), ((), ())), preferred_element_type=jnp.float32
                )
                scores = scores.reshape(2, BLOCK, -1) * FACTOR + bias[blk, :, cut][None]
                parts.append((cut, scores))
                highest = jnp.max(scores, axis=-1, keepdims=True)
                top = highest if top is None else jnp.maximum(top, highest)
            mixed = jnp.zeros((2 * BLOCK, 2 * DIM), jnp.float32)
            for cut, scores in parts:
                weights = jnp.exp2(scores - top).astype(jnp.bfloat16).reshape(2 * BLOCK, -1)
                summed = jnp.concatenate([values[cut], jnp.ones_like(values[cut])], 1)
                mixed += lax.dot_general(
                    weights, summed, (((1,), (0,)), ((), ())), preferred_element_type=jnp.float32
                )
            mixed = (mixed[:, :DIM] / mixed[:, DIM:]).astype(jnp.bfloat16).reshape(2, BLOCK, DIM)
            for u in range(2):
                outb[i, at, u * DIM:(u + 1) * DIM] = mixed[u]

    services = (
        ((lambda: early_tick(0),), (lambda: late_tick(0),), (), (lambda: early_tick(1), lambda: finish(1))),
        ((lambda: late_tick(1),), (), (), (lambda: early_tick(2), lambda: finish(2))),
        ((lambda: late_tick(2),), (), (), (lambda: early_tick(3), lambda: finish(3))),
        ((), (), (), ()),
    )

    for h in range(HEADS_KV):

        def step(seg, _):
            i = h * SEG + seg
            attend(i, h, seg)
            if h < SWAP:
                out(i).start()
            else:
                keep(i).start()
                mid(i, outb).start()

            for at in range(SEG):
                if services[h][at]:

                    @pl.when(seg == at)
                    def _():
                        for service in services[h][at]:
                            service()

            return 0

        lax.fori_loop(0, SEG, step, 0)

    def pass_on(i, _):
        out(i).wait_recv()
        mid(i, recv_out).start()
        return 0

    lax.fori_loop(0, SENT, pass_on, 0)

    for copy in swap_kv():
        copy.wait_send()
    for seg in range(SEG):
        swap_q(seg).wait_send()

    for h in range(HEADS_KV):
        for d in (1, 2, 3):
            pl.when(z < RING - 1)(chain(h, d).wait_send)
        pl.when(z >= RING - 3)(cross(h).wait_send)
        at_z(RING - 1, wrap(h).wait_send)
        pl.when((z == RING - 2) | (z == RING - 3))(stride_one(h).wait_send)
        at_z(3, stride_two(h, 2).wait_send)
        at_z(2, stride_two(h, 3).wait_send)
        for d in range(4):
            sib(h, d).wait_send()

    def drain_kept(i, _):
        keep(i).wait()
        mid(i, outb).wait()
        return 0

    lax.fori_loop(SENT, STEPS, drain_kept, 0)

    def drain_sent(i, _):
        out(i).wait_send()
        mid(i, recv_out).wait()
        return 0

    lax.fori_loop(0, SENT, drain_sent, 0)


def place_kernel(plan, own, side, placed, zeros, sems):
    me = lax.axis_index("ctx")
    core = lax.rem(me, 2)
    first = me // 2 * 4
    count = jnp.int32(0)
    for j in range(4):
        count += (plan[first + j] == me).astype(jnp.int32)
    zeros[...] = jnp.zeros_like(zeros)
    skip = jnp.where(core == 0, 0, 3 - count)

    def each(i, _):
        cols = pl.ds(pl.multiple_of(i * SEG_COLS, SEG_COLS), SEG_COLS)
        for j in range(3):
            to = placed.at[pl.ds(j * BLOCK, BLOCK), cols]
            at = j + skip
            own_at = jnp.where(core == 0, at, at - 1)
            is_side = at == jnp.where(core == 0, 2, 0)
            own_rows = pl.ds(pl.multiple_of(jnp.clip(own_at, 0, 1) * BLOCK, BLOCK), BLOCK)
            fill = pltpu.make_async_copy(zeros, to, sems.at[i, j])
            from_side = pltpu.make_async_copy(side.at[i], to, sems.at[i, j])
            from_own = pltpu.make_async_copy(own.at[i, own_rows], to, sems.at[i, j])
            pl.when(j >= count)(fill.start)
            pl.when((j < count) & is_side)(from_side.start)
            pl.when((j < count) & jnp.logical_not(is_side))(from_own.start)
        return 0

    lax.fori_loop(0, STEPS, each, 0)

    def finish(i, _):
        cols = pl.ds(pl.multiple_of(i * SEG_COLS, SEG_COLS), SEG_COLS)
        for j in range(3):
            to = placed.at[pl.ds(j * BLOCK, BLOCK), cols]
            pltpu.make_async_copy(zeros, to, sems.at[i, j]).wait()
        return 0

    lax.fori_loop(0, STEPS, finish, 0)


def body(query_rows, key_rows, value_rows, doc_lengths, rank_plan, tile_mask):
    dma = pltpu.SemaphoreType.DMA
    anywhere = pl.BlockSpec(memory_space=pl.ANY)
    held = pl.BlockSpec(memory_space=pltpu.HBM)
    scalars = pl.BlockSpec(memory_space=pltpu.SMEM)
    pinned = [
        pltpu.with_memory_space_constraint(x, pltpu.HBM)
        for x in (query_rows[0], key_rows[0], value_rows[0], doc_lengths, tile_mask)
    ]
    received, side = pl.pallas_call(
        attention_kernel,
        out_shape=(
            jax.ShapeDtypeStruct((STEPS, ROWS, SEG_COLS), jnp.bfloat16),
            jax.ShapeDtypeStruct((STEPS, BLOCK, SEG_COLS), jnp.bfloat16),
        ),
        in_specs=[held] * 5,
        out_specs=(anywhere, anywhere),
        scratch_shapes=[
            [pltpu.VMEM((ROWS, HEAD_COLS), jnp.bfloat16)] * HEADS_KV,
            [pltpu.VMEM((SLOTS, 2, ROWS, DIM), jnp.bfloat16)] * HEADS_KV,
            pltpu.VMEM((STEPS, ROWS, SEG_COLS), jnp.bfloat16),
            pltpu.VMEM((2, BLOCK, BAND), jnp.float32),
            pltpu.SMEM((8, tile_mask.shape[1]), jnp.int32),
            pltpu.SMEM(doc_lengths.shape, jnp.int32),
            dma((SWAP,)), dma((SWAP,)), dma((SWAP,)), dma, dma,
            dma((2 + SEG,)), dma((2 + SEG,)),
            dma((HEADS_KV, 3)), dma((HEADS_KV, 3)),
            dma((HEADS_KV, 3)), dma((HEADS_KV, 3)), dma((HEADS_KV,)), dma((HEADS_KV,)),
            dma((HEADS_KV, 4)), dma((HEADS_KV, 4)),
            dma((SENT,)), dma((SENT,)),
            dma((STEPS,)), dma((STEPS,)), dma((STEPS - SENT,)),
        ],
        compiler_params=pltpu.CompilerParams(
            collective_id=0, has_side_effects=True, vmem_limit_bytes=48 * 1024 * 1024
        ),
        name="attention",
    )(*pinned)
    placed = pl.pallas_call(
        place_kernel,
        out_shape=jax.ShapeDtypeStruct((3 * BLOCK, WIDTH), jnp.bfloat16),
        in_specs=[scalars, anywhere, anywhere],
        out_specs=held,
        compiler_params=pltpu.CompilerParams(vmem_limit_bytes=8 * 1024 * 1024),
        scratch_shapes=[pltpu.VMEM((BLOCK, SEG_COLS), jnp.bfloat16), dma((STEPS, 3))],
        name="place",
    )(rank_plan, received, side)
    return placed[None]


def solution(mesh):
    placed = (
        P("section", "ctx", None),
        P("section", "ctx", None),
        P("section", "ctx", None),
        P(),
        P(),
        P(),
    )
    return jax.shard_map(
        body, mesh=mesh, in_specs=placed, out_specs=P("section", "ctx", None), check_vma=False
    )
```

```python
import math

import jax
import jax.numpy as jnp
from jax import lax
from jax.experimental import pallas as pl
from jax.experimental.pallas import tpu as pltpu
from jax.sharding import PartitionSpec as P

BLOCK = 128
ROWS = 256
HEADS_KV = 4
GROUP = 8
DIM = 128
WIDTH = HEADS_KV * GROUP * DIM
HEAD_COLS = GROUP * DIM
RING = 8
BAND = 13 * BLOCK
PART = 4 * BLOCK
SLOTS = 10
SEG = 4
SEG_COLS = HEAD_COLS // SEG
SWAP = HEADS_KV - 1
STEPS = HEADS_KV * SEG
SENT = SWAP * SEG
FACTOR = DIM**-0.5 * math.log2(math.e)
NEG = -1e30


def attention_kernel(
    q_hbm, k_hbm, v_hbm, lengths_hbm, mask_hbm,
    recv_out, side_out,
    qbuf, kv, outb, bias, marks, lengths,
    q_sem, k_sem, v_sem, mark_sem, length_sem,
    swap_send, swap_recv,
    chain_send, chain_recv,
    hop_send, hop_recv, cross_send, cross_recv,
    sib_send, sib_recv,
    out_send, out_recv,
    mid_send, mid_recv, keep_sem,
):
    me = lax.axis_index("ctx")
    section = lax.axis_index("section")
    core = lax.rem(me, 2)
    chip = me // 2
    z = lax.rem(chip, RING)
    ring = chip // RING
    rings = lax.axis_size("ctx") // (2 * RING)

    def device(ring_at, z_at, core_at):
        return {"ctx": (ring_at * RING + z_at) * 2 + core_at, "section": section}

    z_next = lax.rem(z + 1, RING)
    z_prev = lax.rem(z + RING - 1, RING)
    sibling = device(ring, z, 1 - core)
    ahead = device(ring, z_next, core)
    behind = device(ring, z_prev, core)
    over = device(lax.rem(ring + 1, rings), z, core)
    under = device(lax.rem(ring + rings - 1, rings), z, core)
    partner = {"ctx": me, "section": 1 - section}

    def held(d):
        return (3 - d) * 2 + core

    def remote(src, dst, send, recv, to):
        return pltpu.make_async_remote_copy(
            src_ref=src, dst_ref=dst, send_sem=send, recv_sem=recv,
            device_id=to, device_id_type=pl.DeviceIdType.MESH,
        )

    def load_q(h):
        cols = pl.ds(pl.multiple_of(h * HEAD_COLS, HEAD_COLS), HEAD_COLS)
        return pltpu.make_async_copy(q_hbm.at[:, cols], qbuf[h], q_sem.at[h])

    def load_kv(h):
        cols = pl.ds(pl.multiple_of(h * DIM, DIM), DIM)
        return (
            pltpu.make_async_copy(k_hbm.at[:, cols], kv[h].at[6 + core, 0], k_sem.at[h]),
            pltpu.make_async_copy(v_hbm.at[:, cols], kv[h].at[6 + core, 1], v_sem.at[h]),
        )

    mark_row = chip * 4 // 8 * 8
    load_marks = pltpu.make_async_copy(
        mask_hbm.at[pl.ds(pl.multiple_of(mark_row, 8), 8)], marks, mark_sem
    )

    load_lengths = pltpu.make_async_copy(lengths_hbm, lengths, length_sem)

    def swap_q(seg):
        cols = pl.ds(SWAP * HEAD_COLS + seg * SEG_COLS, SEG_COLS)
        to = pl.ds(seg * SEG_COLS, SEG_COLS)
        return remote(q_hbm.at[:, cols], qbuf[SWAP].at[:, to],
                      swap_send.at[2 + seg], swap_recv.at[2 + seg], partner)

    def swap_kv():
        cols = pl.ds(SWAP * DIM, DIM)
        return (
            remote(k_hbm.at[:, cols], kv[SWAP].at[6 + core, 0],
                   swap_send.at[0], swap_recv.at[0], partner),
            remote(v_hbm.at[:, cols], kv[SWAP].at[6 + core, 1],
                   swap_send.at[1], swap_recv.at[1], partner),
        )

    def chain(h, d):
        return remote(kv[h].at[held(d - 1)], kv[h].at[held(d)],
                      chain_send.at[h, d - 1], chain_recv.at[h, d - 1], ahead)

    def cross(h):
        return remote(kv[h].at[6 + core], kv[h].at[8], cross_send.at[h], cross_recv.at[h], over)

    def wrap(h):
        return remote(kv[h].at[8], kv[h].at[held(1)], chain_send.at[h, 0], chain_recv.at[h, 0], ahead)

    def stride_one(h):
        return remote(kv[h].at[8], kv[h].at[9], hop_send.at[h, 0], hop_recv.at[h, 0],
                      device(ring, lax.rem(z + RING - 3, RING), core))

    def stride_two(h, d):
        return remote(kv[h].at[9], kv[h].at[held(d)], hop_send.at[h, d - 1], hop_recv.at[h, d - 1],
                      device(ring, 0, core))

    def sib(h, d, core_at=core):
        return remote(kv[h].at[(3 - d) * 2 + core], kv[h].at[(3 - d) * 2 + core_at],
                      sib_send.at[h, d], sib_recv.at[h, d], sibling)

    def sib_wait(h, d):
        sib(h, d, 1 - core).wait_recv()

    def out(i):
        return remote(outb.at[i], recv_out.at[i], out_send.at[i], out_recv.at[i], partner)

    def keep(i):
        return pltpu.make_async_copy(outb.at[i], recv_out.at[i], keep_sem.at[i - SENT])

    middle = pl.ds(pl.multiple_of((1 - core) * BLOCK, BLOCK), BLOCK)

    def mid(i, source):
        return remote(source.at[i, middle], side_out.at[i],
                      mid_send.at[i], mid_recv.at[i], sibling)

    def own_ready(h):
        if h < SWAP:
            for copy in load_kv(h):
                copy.wait()
        else:
            for copy in swap_kv():
                copy.wait_recv()

    def at_z(place, *actions):
        @pl.when(z == place)
        def _():
            for action in actions:
                action()

    def ready(n, e):
        if e < 3:

            @pl.when(z < RING - 1)
            def _():
                chain(n, e + 1).start()

        sib(n, e).start()

    def arrive(n, d):
        chain(n, d).wait_recv()
        ready(n, d)

    def arrive_over(n, d):
        if d == 1:
            chain(n, d).wait_recv()
        else:
            at_z(0, stride_two(n, d).wait_recv)
            pl.when(z > 0)(chain(n, d).wait_recv)
        ready(n, d)

    def own(n):
        own_ready(n)

        @pl.when(z >= RING - 3)
        def _():
            cross(n).start()

    def tick(h):
        now = h + 4
        for n in range(HEADS_KV):
            if now == n == 0:
                own(n)
        for d in (3, 2, 1):
            if 0 <= now - d - 1 < HEADS_KV and (now, d) != (4, 3):
                pl.when(z < d)(lambda: arrive_over(now - d - 1, d))
            if 0 <= now - d < HEADS_KV:
                pl.when(z >= d)(lambda: arrive(now - d, d))
        if now < HEADS_KV:
            ready(now, 0)
        if now + 1 < HEADS_KV:
            own(now + 1)
        for n in range(HEADS_KV):
            if now == n + 2:
                at_z(3, stride_one(n).wait_recv, stride_two(n, 2).start)
                at_z(2, stride_one(n).wait_recv, stride_two(n, 3).start)
            if now == n + 1:
                at_z(RING - 1, cross(n).wait_recv, wrap(n).start)

                @pl.when((z == RING - 2) | (z == RING - 3))
                def _():
                    cross(n).wait_recv()
                    stride_one(n).start()

    def finish(n):
        for d in range(4):
            sib_wait(n, d)

        if n < SWAP:
            load_q(n).wait()
        else:
            for seg in range(SEG):
                swap_q(seg).wait_recv()

    for h in range(SWAP):
        for copy in load_kv(h):
            copy.start()
    load_marks.start()
    load_lengths.start()
    for h in range(SWAP):
        load_q(h).start()

    barrier = pltpu.get_barrier_semaphore()
    def greet(other):
        pl.semaphore_signal(barrier, inc=1, device_id=other, device_id_type=pl.DeviceIdType.MESH)

    for other in (sibling, ahead, behind, partner):
        greet(other)
    pairs = ((5, 2), (6, 3), (3, 0), (2, 0))
    for a, b in pairs:
        at_z(a, lambda: greet(device(ring, b, core)))
        at_z(b, lambda: greet(device(ring, a, core)))

    @pl.when(z >= RING - 3)
    def _():
        greet(over)
        greet(under)

    for place in range(RING):
        greeted = 4 + 2 * (place >= RING - 3) + sum(pair.count(place) for pair in pairs)
        at_z(place, lambda: pl.semaphore_wait(barrier, greeted))

    tick(-4)
    for copy in swap_kv():
        copy.start()
    swap_q(0).start()

    load_marks.wait()
    load_lengths.wait()
    first_query = (chip * 4 + core * 2) * BLOCK
    for blk in range(2):
        query = first_query + blk * BLOCK + lax.broadcasted_iota(jnp.int32, (BLOCK, BLOCK), 0)

        def latest(j, carried):
            begin, best = carried
            best = jnp.where(query >= begin, begin, best)
            return begin + lengths[j], best

        _, begin_of = lax.fori_loop(
            0, lengths.shape[0], latest, (jnp.int32(0), jnp.zeros((BLOCK, BLOCK), jnp.int32))
        )
        for j in range(13):
            key_block = chip * 4 + core * 2 + blk - 12 + j
            mark = marks[chip * 4 - mark_row + core * 2 + blk, jnp.maximum(key_block, 0)]
            key = key_block * BLOCK + lax.broadcasted_iota(jnp.int32, (BLOCK, BLOCK), 1)
            seen = (key <= query) & (key >= begin_of) & (mark > 0)
            bias[blk, :, j * BLOCK:(j + 1) * BLOCK] = jnp.where(seen, 0.0, NEG)

    for h in (-3, -2, -1):
        tick(h)
        swap_q(h + 4).start()

    def early_tick(h):
        pl.when(z < 3)(lambda: tick(h))

    def late_tick(h):
        pl.when(z >= 3)(lambda: tick(h))

    pl.when(z < 3)(lambda: arrive_over(0, 3))
    finish(0)

    def attend(i, h, seg):
        for blk in range(2):
            at = pl.ds(blk * BLOCK, BLOCK)
            cols = [pl.ds(pl.multiple_of(seg * SEG_COLS + u * DIM, DIM), DIM) for u in range(2)]
            queries = jnp.concatenate([qbuf[h][at, c] for c in cols], 0)
            window = pl.ds(core, 7)
            keys = kv[h][window, 0].reshape(7 * ROWS, DIM)[blk * BLOCK:blk * BLOCK + BAND]
            values = kv[h][window, 1].reshape(7 * ROWS, DIM)[blk * BLOCK:blk * BLOCK + BAND]
            parts = []
            top = None
            for first in range(0, BAND, PART):
                cut = slice(first, min(first + PART, BAND))
                scores = lax.dot_general(
                    queries, keys[cut], (((1,), (1,)), ((), ())), preferred_element_type=jnp.float32
                )
                scores = scores.reshape(2, BLOCK, -1) * FACTOR + bias[blk, :, cut][None]
                parts.append((cut, scores))
                highest = jnp.max(scores, axis=-1, keepdims=True)
                top = highest if top is None else jnp.maximum(top, highest)
            mixed = jnp.zeros((2 * BLOCK, 2 * DIM), jnp.float32)
            for cut, scores in parts:
                weights = jnp.exp2(scores - top).astype(jnp.bfloat16).reshape(2 * BLOCK, -1)
                summed = jnp.concatenate([values[cut], jnp.ones_like(values[cut])], 1)
                mixed += lax.dot_general(
                    weights, summed, (((1,), (0,)), ((), ())), preferred_element_type=jnp.float32
                )
            mixed = (mixed[:, :DIM] / mixed[:, DIM:]).astype(jnp.bfloat16).reshape(2, BLOCK, DIM)
            for u in range(2):
                outb[i, at, u * DIM:(u + 1) * DIM] = mixed[u]

    services = (
        ((lambda: early_tick(0),), (lambda: late_tick(0),), (), (lambda: early_tick(1), lambda: finish(1))),
        ((lambda: late_tick(1),), (), (), (lambda: early_tick(2), lambda: finish(2))),
        ((lambda: late_tick(2),), (), (), (lambda: early_tick(3), lambda: finish(3))),
        ((), (), (), ()),
    )

    for h in range(HEADS_KV):

        def step(seg, _):
            i = h * SEG + seg
            attend(i, h, seg)
            if h < SWAP:
                out(i).start()
            else:
                keep(i).start()
                mid(i, outb).start()

            for at in range(SEG):
                if services[h][at]:

                    @pl.when(seg == at)
                    def _():
                        for service in services[h][at]:
                            service()

            return 0

        lax.fori_loop(0, SEG, step, 0)

    def pass_on(i, _):
        out(i).wait_recv()
        mid(i, recv_out).start()
        return 0

    lax.fori_loop(0, SENT, pass_on, 0)

    for copy in swap_kv():
        copy.wait_send()
    for seg in range(SEG):
        swap_q(seg).wait_send()

    for h in range(HEADS_KV):
        for d in (1, 2, 3):
            pl.when(z < RING - 1)(chain(h, d).wait_send)
        pl.when(z >= RING - 3)(cross(h).wait_send)
        at_z(RING - 1, wrap(h).wait_send)
        pl.when((z == RING - 2) | (z == RING - 3))(stride_one(h).wait_send)
        at_z(3, stride_two(h, 2).wait_send)
        at_z(2, stride_two(h, 3).wait_send)
        for d in range(4):
            sib(h, d).wait_send()

    def drain_kept(i, _):
        keep(i).wait()
        mid(i, outb).wait()
        return 0

    lax.fori_loop(SENT, STEPS, drain_kept, 0)

    def drain_sent(i, _):
        out(i).wait_send()
        mid(i, recv_out).wait()
        return 0

    lax.fori_loop(0, SENT, drain_sent, 0)


def place_kernel(plan, own, side, placed, zeros, sems):
    me = lax.axis_index("ctx")
    core = lax.rem(me, 2)
    first = me // 2 * 4
    count = jnp.int32(0)
    for j in range(4):
        count += (plan[first + j] == me).astype(jnp.int32)
    zeros[...] = jnp.zeros_like(zeros)
    skip = jnp.where(core == 0, 0, 3 - count)

    def each(i, _):
        cols = pl.ds(pl.multiple_of(i * SEG_COLS, SEG_COLS), SEG_COLS)
        for j in range(3):
            to = placed.at[pl.ds(j * BLOCK, BLOCK), cols]
            at = j + skip
            own_at = jnp.where(core == 0, at, at - 1)
            is_side = at == jnp.where(core == 0, 2, 0)
            own_rows = pl.ds(pl.multiple_of(jnp.clip(own_at, 0, 1) * BLOCK, BLOCK), BLOCK)
            fill = pltpu.make_async_copy(zeros, to, sems.at[i, j])
            from_side = pltpu.make_async_copy(side.at[i], to, sems.at[i, j])
            from_own = pltpu.make_async_copy(own.at[i, own_rows], to, sems.at[i, j])
            pl.when(j >= count)(fill.start)
            pl.when((j < count) & is_side)(from_side.start)
            pl.when((j < count) & jnp.logical_not(is_side))(from_own.start)
        return 0

    lax.fori_loop(0, STEPS, each, 0)

    def finish(i, _):
        cols = pl.ds(pl.multiple_of(i * SEG_COLS, SEG_COLS), SEG_COLS)
        for j in range(3):
            to = placed.at[pl.ds(j * BLOCK, BLOCK), cols]
            pltpu.make_async_copy(zeros, to, sems.at[i, j]).wait()
        return 0

    lax.fori_loop(0, STEPS, finish, 0)


def body(query_rows, key_rows, value_rows, doc_lengths, rank_plan, tile_mask):
    dma = pltpu.SemaphoreType.DMA
    anywhere = pl.BlockSpec(memory_space=pl.ANY)
    held = pl.BlockSpec(memory_space=pltpu.HBM)
    scalars = pl.BlockSpec(memory_space=pltpu.SMEM)
    pinned = [
        pltpu.with_memory_space_constraint(x, pltpu.HBM)
        for x in (query_rows[0], key_rows[0], value_rows[0], doc_lengths, tile_mask)
    ]
    received, side = pl.pallas_call(
        attention_kernel,
        out_shape=(
            jax.ShapeDtypeStruct((STEPS, ROWS, SEG_COLS), jnp.bfloat16),
            jax.ShapeDtypeStruct((STEPS, BLOCK, SEG_COLS), jnp.bfloat16),
        ),
        in_specs=[held] * 5,
        out_specs=(anywhere, anywhere),
        scratch_shapes=[
            [pltpu.VMEM((ROWS, HEAD_COLS), jnp.bfloat16)] * HEADS_KV,
            [pltpu.VMEM((SLOTS, 2, ROWS, DIM), jnp.bfloat16)] * HEADS_KV,
            pltpu.VMEM((STEPS, ROWS, SEG_COLS), jnp.bfloat16),
            pltpu.VMEM((2, BLOCK, BAND), jnp.float32),
            pltpu.SMEM((8, tile_mask.shape[1]), jnp.int32),
            pltpu.SMEM(doc_lengths.shape, jnp.int32),
            dma((SWAP,)), dma((SWAP,)), dma((SWAP,)), dma, dma,
            dma((2 + SEG,)), dma((2 + SEG,)),
            dma((HEADS_KV, 3)), dma((HEADS_KV, 3)),
            dma((HEADS_KV, 3)), dma((HEADS_KV, 3)), dma((HEADS_KV,)), dma((HEADS_KV,)),
            dma((HEADS_KV, 4)), dma((HEADS_KV, 4)),
            dma((SENT,)), dma((SENT,)),
            dma((STEPS,)), dma((STEPS,)), dma((STEPS - SENT,)),
        ],
        compiler_params=pltpu.CompilerParams(
            collective_id=0, has_side_effects=True, vmem_limit_bytes=48 * 1024 * 1024
        ),
        name="attention",
    )(*pinned)
    placed = pl.pallas_call(
        place_kernel,
        out_shape=jax.ShapeDtypeStruct((3 * BLOCK, WIDTH), jnp.bfloat16),
        in_specs=[scalars, anywhere, anywhere],
        out_specs=held,
        compiler_params=pltpu.CompilerParams(vmem_limit_bytes=8 * 1024 * 1024),
        scratch_shapes=[pltpu.VMEM((BLOCK, SEG_COLS), jnp.bfloat16), dma((STEPS, 3))],
        name="place",
    )(rank_plan, received, side)
    return placed[None]


def solution(mesh):
    placed = (
        P("section", "ctx", None),
        P("section", "ctx", None),
        P("section", "ctx", None),
        P(),
        P(),
        P(),
    )
    return jax.shard_map(
        body, mesh=mesh, in_specs=placed, out_specs=P("section", "ctx", None), check_vma=False
    )
```

```python
import math

import jax
import jax.numpy as jnp
from jax import lax
from jax.experimental import pallas as pl
from jax.experimental.pallas import tpu as pltpu
from jax.sharding import PartitionSpec as P

BLOCK = 128
ROWS = 256
HEADS_KV = 4
GROUP = 8
DIM = 128
WIDTH = HEADS_KV * GROUP * DIM
HEAD_COLS = GROUP * DIM
RING = 8
BAND = 13 * BLOCK
PART = 4 * BLOCK
SLOTS = 10
SEG = 4
SEG_COLS = HEAD_COLS // SEG
SWAP = HEADS_KV - 1
STEPS = HEADS_KV * SEG
SENT = SWAP * SEG
FACTOR = DIM**-0.5 * math.log2(math.e)
NEG = -1e30


def attention_kernel(
    q_hbm, k_hbm, v_hbm, lengths_hbm, mask_hbm,
    recv_out, side_out,
    qbuf, kv, outb, bias, marks, lengths,
    q_sem, k_sem, v_sem, mark_sem, length_sem,
    swap_send, swap_recv,
    chain_send, chain_recv,
    hop_send, hop_recv, cross_send, cross_recv,
    sib_send, sib_recv,
    out_send, out_recv,
    mid_send, mid_recv, keep_sem,
):
    me = lax.axis_index("ctx")
    section = lax.axis_index("section")
    core = lax.rem(me, 2)
    chip = me // 2
    z = lax.rem(chip, RING)
    ring = chip // RING
    rings = lax.axis_size("ctx") // (2 * RING)

    def device(ring_at, z_at, core_at):
        return {"ctx": (ring_at * RING + z_at) * 2 + core_at, "section": section}

    z_next = lax.rem(z + 1, RING)
    z_prev = lax.rem(z + RING - 1, RING)
    sibling = device(ring, z, 1 - core)
    ahead = device(ring, z_next, core)
    behind = device(ring, z_prev, core)
    over = device(lax.rem(ring + 1, rings), z, core)
    under = device(lax.rem(ring + rings - 1, rings), z, core)
    partner = {"ctx": me, "section": 1 - section}

    def held(d):
        return (3 - d) * 2 + core

    def remote(src, dst, send, recv, to):
        return pltpu.make_async_remote_copy(
            src_ref=src, dst_ref=dst, send_sem=send, recv_sem=recv,
            device_id=to, device_id_type=pl.DeviceIdType.MESH,
        )

    def load_q(h):
        cols = pl.ds(pl.multiple_of(h * HEAD_COLS, HEAD_COLS), HEAD_COLS)
        return pltpu.make_async_copy(q_hbm.at[:, cols], qbuf[h], q_sem.at[h])

    def load_kv(h):
        cols = pl.ds(pl.multiple_of(h * DIM, DIM), DIM)
        return (
            pltpu.make_async_copy(k_hbm.at[:, cols], kv[h].at[6 + core, 0], k_sem.at[h]),
            pltpu.make_async_copy(v_hbm.at[:, cols], kv[h].at[6 + core, 1], v_sem.at[h]),
        )

    mark_row = chip * 4 // 8 * 8
    load_marks = pltpu.make_async_copy(
        mask_hbm.at[pl.ds(pl.multiple_of(mark_row, 8), 8)], marks, mark_sem
    )

    load_lengths = pltpu.make_async_copy(lengths_hbm, lengths, length_sem)

    def swap_q(seg):
        cols = pl.ds(SWAP * HEAD_COLS + seg * SEG_COLS, SEG_COLS)
        to = pl.ds(seg * SEG_COLS, SEG_COLS)
        return remote(q_hbm.at[:, cols], qbuf[SWAP].at[:, to],
                      swap_send.at[2 + seg], swap_recv.at[2 + seg], partner)

    def swap_kv():
        cols = pl.ds(SWAP * DIM, DIM)
        return (
            remote(k_hbm.at[:, cols], kv[SWAP].at[6 + core, 0],
                   swap_send.at[0], swap_recv.at[0], partner),
            remote(v_hbm.at[:, cols], kv[SWAP].at[6 + core, 1],
                   swap_send.at[1], swap_recv.at[1], partner),
        )

    def chain(h, d):
        return remote(kv[h].at[held(d - 1)], kv[h].at[held(d)],
                      chain_send.at[h, d - 1], chain_recv.at[h, d - 1], ahead)

    def cross(h):
        return remote(kv[h].at[6 + core], kv[h].at[8], cross_send.at[h], cross_recv.at[h], over)

    def wrap(h):
        return remote(kv[h].at[8], kv[h].at[held(1)], chain_send.at[h, 0], chain_recv.at[h, 0], ahead)

    def stride_one(h):
        return remote(kv[h].at[8], kv[h].at[9], hop_send.at[h, 0], hop_recv.at[h, 0],
                      device(ring, lax.rem(z + RING - 3, RING), core))

    def stride_two(h, d):
        return remote(kv[h].at[9], kv[h].at[held(d)], hop_send.at[h, d - 1], hop_recv.at[h, d - 1],
                      device(ring, 0, core))

    def sib(h, d, core_at=core):
        return remote(kv[h].at[(3 - d) * 2 + core], kv[h].at[(3 - d) * 2 + core_at],
                      sib_send.at[h, d], sib_recv.at[h, d], sibling)

    def sib_wait(h, d):
        sib(h, d, 1 - core).wait_recv()

    def out(i):
        return remote(outb.at[i], recv_out.at[i], out_send.at[i], out_recv.at[i], partner)

    def keep(i):
        return pltpu.make_async_copy(outb.at[i], recv_out.at[i], keep_sem.at[i - SENT])

    middle = pl.ds(pl.multiple_of((1 - core) * BLOCK, BLOCK), BLOCK)

    def mid(i, source):
        return remote(source.at[i, middle], side_out.at[i],
                      mid_send.at[i], mid_recv.at[i], sibling)

    def own_ready(h):
        if h < SWAP:
            for copy in load_kv(h):
                copy.wait()
        else:
            for copy in swap_kv():
                copy.wait_recv()

    def at_z(place, *actions):
        @pl.when(z == place)
        def _():
            for action in actions:
                action()

    def ready(n, e):
        if e < 3:

            @pl.when(z < RING - 1)
            def _():
                chain(n, e + 1).start()

        sib(n, e).start()

    def arrive(n, d):
        chain(n, d).wait_recv()
        ready(n, d)

    def arrive_over(n, d):
        if d == 1:
            chain(n, d).wait_recv()
        else:
            at_z(0, stride_two(n, d).wait_recv)
            pl.when(z > 0)(chain(n, d).wait_recv)
        ready(n, d)

    def own(n):
        own_ready(n)

        @pl.when(z >= RING - 3)
        def _():
            cross(n).start()

    def tick(h):
        now = h + 4
        for n in range(HEADS_KV):
            if now == n == 0:
                own(n)
        for d in (3, 2, 1):
            if 0 <= now - d - 1 < HEADS_KV and (now, d) != (4, 3):
                pl.when(z < d)(lambda: arrive_over(now - d - 1, d))
            if 0 <= now - d < HEADS_KV:
                pl.when(z >= d)(lambda: arrive(now - d, d))
        if 0 < now < HEADS_KV:
            own(now)
        if now < HEADS_KV:
            ready(now, 0)
        for n in range(HEADS_KV):
            if now == n + 2:
                at_z(3, stride_one(n).wait_recv, stride_two(n, 2).start)
                at_z(2, stride_one(n).wait_recv, stride_two(n, 3).start)
            if now == n + 1:
                at_z(RING - 1, cross(n).wait_recv, wrap(n).start)

                @pl.when((z == RING - 2) | (z == RING - 3))
                def _():
                    cross(n).wait_recv()
                    stride_one(n).start()

    def finish(n):
        for d in range(4):
            sib_wait(n, d)

        if n < SWAP:
            load_q(n).wait()
        else:
            for seg in range(SEG):
                swap_q(seg).wait_recv()

    for h in range(SWAP):
        for copy in load_kv(h):
            copy.start()
    load_marks.start()
    load_lengths.start()
    for h in range(SWAP):
        load_q(h).start()

    barrier = pltpu.get_barrier_semaphore()
    def greet(other):
        pl.semaphore_signal(barrier, inc=1, device_id=other, device_id_type=pl.DeviceIdType.MESH)

    for other in (sibling, ahead, behind, partner):
        greet(other)
    pairs = ((5, 2), (6, 3), (3, 0), (2, 0))
    for a, b in pairs:
        at_z(a, lambda: greet(device(ring, b, core)))
        at_z(b, lambda: greet(device(ring, a, core)))

    @pl.when(z >= RING - 3)
    def _():
        greet(over)
        greet(under)

    for place in range(RING):
        greeted = 4 + 2 * (place >= RING - 3) + sum(pair.count(place) for pair in pairs)
        at_z(place, lambda: pl.semaphore_wait(barrier, greeted))

    tick(-4)
    for copy in swap_kv():
        copy.start()
    swap_q(0).start()

    load_marks.wait()
    load_lengths.wait()
    first_query = (chip * 4 + core * 2) * BLOCK
    for blk in range(2):
        query = first_query + blk * BLOCK + lax.broadcasted_iota(jnp.int32, (BLOCK, BLOCK), 0)

        def latest(j, carried):
            begin, best = carried
            best = jnp.where(query >= begin, begin, best)
            return begin + lengths[j], best

        _, begin_of = lax.fori_loop(
            0, lengths.shape[0], latest, (jnp.int32(0), jnp.zeros((BLOCK, BLOCK), jnp.int32))
        )
        for j in range(13):
            key_block = chip * 4 + core * 2 + blk - 12 + j
            mark = marks[chip * 4 - mark_row + core * 2 + blk, jnp.maximum(key_block, 0)]
            key = key_block * BLOCK + lax.broadcasted_iota(jnp.int32, (BLOCK, BLOCK), 1)
            seen = (key <= query) & (key >= begin_of) & (mark > 0)
            bias[blk, :, j * BLOCK:(j + 1) * BLOCK] = jnp.where(seen, 0.0, NEG)

    for h in (-3, -2, -1):
        tick(h)
        swap_q(h + 4).start()

    def early_tick(h):
        pl.when(z < 3)(lambda: tick(h))

    def late_tick(h):
        pl.when(z >= 3)(lambda: tick(h))

    pl.when(z < 3)(lambda: arrive_over(0, 3))
    finish(0)

    def attend(i, h, seg):
        for blk in range(2):
            at = pl.ds(blk * BLOCK, BLOCK)
            cols = [pl.ds(pl.multiple_of(seg * SEG_COLS + u * DIM, DIM), DIM) for u in range(2)]
            queries = jnp.concatenate([qbuf[h][at, c] for c in cols], 0)
            window = pl.ds(core, 7)
            keys = kv[h][window, 0].reshape(7 * ROWS, DIM)[blk * BLOCK:blk * BLOCK + BAND]
            values = kv[h][window, 1].reshape(7 * ROWS, DIM)[blk * BLOCK:blk * BLOCK + BAND]
            parts = []
            top = None
            for first in range(0, BAND, PART):
                cut = slice(first, min(first + PART, BAND))
                scores = lax.dot_general(
                    queries, keys[cut], (((1,), (1,)), ((), ())), preferred_element_type=jnp.float32
                )
                scores = scores.reshape(2, BLOCK, -1) * FACTOR + bias[blk, :, cut][None]
                parts.append((cut, scores))
                highest = jnp.max(scores, axis=-1, keepdims=True)
                top = highest if top is None else jnp.maximum(top, highest)
            mixed = jnp.zeros((2 * BLOCK, 2 * DIM), jnp.float32)
            for cut, scores in parts:
                weights = jnp.exp2(scores - top).astype(jnp.bfloat16).reshape(2 * BLOCK, -1)
                summed = jnp.concatenate([values[cut], jnp.ones_like(values[cut])], 1)
                mixed += lax.dot_general(
                    weights, summed, (((1,), (0,)), ((), ())), preferred_element_type=jnp.float32
                )
            mixed = (mixed[:, :DIM] / mixed[:, DIM:]).astype(jnp.bfloat16).reshape(2, BLOCK, DIM)
            for u in range(2):
                outb[i, at, u * DIM:(u + 1) * DIM] = mixed[u]

    services = (
        ((lambda: early_tick(0),), (lambda: late_tick(0),), (), (lambda: early_tick(1), lambda: finish(1))),
        ((lambda: late_tick(1),), (), (), (lambda: early_tick(2), lambda: finish(2))),
        ((lambda: late_tick(2),), (), (), (lambda: early_tick(3), lambda: finish(3))),
        ((), (), (), ()),
    )

    for h in range(HEADS_KV):

        def step(seg, _):
            i = h * SEG + seg
            attend(i, h, seg)
            if h < SWAP:
                out(i).start()
            else:
                keep(i).start()
                mid(i, outb).start()

            for at in range(SEG):
                if services[h][at]:

                    @pl.when(seg == at)
                    def _():
                        for service in services[h][at]:
                            service()

            return 0

        lax.fori_loop(0, SEG, step, 0)

    def pass_on(i, _):
        out(i).wait_recv()
        mid(i, recv_out).start()
        return 0

    lax.fori_loop(0, SENT, pass_on, 0)

    for copy in swap_kv():
        copy.wait_send()
    for seg in range(SEG):
        swap_q(seg).wait_send()

    for h in range(HEADS_KV):
        for d in (1, 2, 3):
            pl.when(z < RING - 1)(chain(h, d).wait_send)
        pl.when(z >= RING - 3)(cross(h).wait_send)
        at_z(RING - 1, wrap(h).wait_send)
        pl.when((z == RING - 2) | (z == RING - 3))(stride_one(h).wait_send)
        at_z(3, stride_two(h, 2).wait_send)
        at_z(2, stride_two(h, 3).wait_send)
        for d in range(4):
            sib(h, d).wait_send()

    def drain_kept(i, _):
        keep(i).wait()
        mid(i, outb).wait()
        return 0

    lax.fori_loop(SENT, STEPS, drain_kept, 0)

    def drain_sent(i, _):
        out(i).wait_send()
        mid(i, recv_out).wait()
        return 0

    lax.fori_loop(0, SENT, drain_sent, 0)


def place_kernel(plan, own, side, placed, zeros, sems):
    me = lax.axis_index("ctx")
    core = lax.rem(me, 2)
    first = me // 2 * 4
    count = jnp.int32(0)
    for j in range(4):
        count += (plan[first + j] == me).astype(jnp.int32)
    zeros[...] = jnp.zeros_like(zeros)
    skip = jnp.where(core == 0, 0, 3 - count)

    def each(i, _):
        cols = pl.ds(pl.multiple_of(i * SEG_COLS, SEG_COLS), SEG_COLS)
        for j in range(3):
            to = placed.at[pl.ds(j * BLOCK, BLOCK), cols]
            at = j + skip
            own_at = jnp.where(core == 0, at, at - 1)
            is_side = at == jnp.where(core == 0, 2, 0)
            own_rows = pl.ds(pl.multiple_of(jnp.clip(own_at, 0, 1) * BLOCK, BLOCK), BLOCK)
            fill = pltpu.make_async_copy(zeros, to, sems.at[i, j])
            from_side = pltpu.make_async_copy(side.at[i], to, sems.at[i, j])
            from_own = pltpu.make_async_copy(own.at[i, own_rows], to, sems.at[i, j])
            pl.when(j >= count)(fill.start)
            pl.when((j < count) & is_side)(from_side.start)
            pl.when((j < count) & jnp.logical_not(is_side))(from_own.start)
        return 0

    lax.fori_loop(0, STEPS, each, 0)

    def finish(i, _):
        cols = pl.ds(pl.multiple_of(i * SEG_COLS, SEG_COLS), SEG_COLS)
        for j in range(3):
            to = placed.at[pl.ds(j * BLOCK, BLOCK), cols]
            pltpu.make_async_copy(zeros, to, sems.at[i, j]).wait()
        return 0

    lax.fori_loop(0, STEPS, finish, 0)


def body(query_rows, key_rows, value_rows, doc_lengths, rank_plan, tile_mask):
    dma = pltpu.SemaphoreType.DMA
    anywhere = pl.BlockSpec(memory_space=pl.ANY)
    held = pl.BlockSpec(memory_space=pltpu.HBM)
    scalars = pl.BlockSpec(memory_space=pltpu.SMEM)
    pinned = [
        pltpu.with_memory_space_constraint(x, pltpu.HBM)
        for x in (query_rows[0], key_rows[0], value_rows[0], doc_lengths, tile_mask)
    ]
    received, side = pl.pallas_call(
        attention_kernel,
        out_shape=(
            jax.ShapeDtypeStruct((STEPS, ROWS, SEG_COLS), jnp.bfloat16),
            jax.ShapeDtypeStruct((STEPS, BLOCK, SEG_COLS), jnp.bfloat16),
        ),
        in_specs=[held] * 5,
        out_specs=(anywhere, anywhere),
        scratch_shapes=[
            [pltpu.VMEM((ROWS, HEAD_COLS), jnp.bfloat16)] * HEADS_KV,
            [pltpu.VMEM((SLOTS, 2, ROWS, DIM), jnp.bfloat16)] * HEADS_KV,
            pltpu.VMEM((STEPS, ROWS, SEG_COLS), jnp.bfloat16),
            pltpu.VMEM((2, BLOCK, BAND), jnp.float32),
            pltpu.SMEM((8, tile_mask.shape[1]), jnp.int32),
            pltpu.SMEM(doc_lengths.shape, jnp.int32),
            dma((SWAP,)), dma((SWAP,)), dma((SWAP,)), dma, dma,
            dma((2 + SEG,)), dma((2 + SEG,)),
            dma((HEADS_KV, 3)), dma((HEADS_KV, 3)),
            dma((HEADS_KV, 3)), dma((HEADS_KV, 3)), dma((HEADS_KV,)), dma((HEADS_KV,)),
            dma((HEADS_KV, 4)), dma((HEADS_KV, 4)),
            dma((SENT,)), dma((SENT,)),
            dma((STEPS,)), dma((STEPS,)), dma((STEPS - SENT,)),
        ],
        compiler_params=pltpu.CompilerParams(
            collective_id=0, has_side_effects=True, vmem_limit_bytes=48 * 1024 * 1024
        ),
        name="attention",
    )(*pinned)
    placed = pl.pallas_call(
        place_kernel,
        out_shape=jax.ShapeDtypeStruct((3 * BLOCK, WIDTH), jnp.bfloat16),
        in_specs=[scalars, anywhere, anywhere],
        out_specs=held,
        compiler_params=pltpu.CompilerParams(vmem_limit_bytes=8 * 1024 * 1024),
        scratch_shapes=[pltpu.VMEM((BLOCK, SEG_COLS), jnp.bfloat16), dma((STEPS, 3))],
        name="place",
    )(rank_plan, received, side)
    return placed[None]


def solution(mesh):
    placed = (
        P("section", "ctx", None),
        P("section", "ctx", None),
        P("section", "ctx", None),
        P(),
        P(),
        P(),
    )
    return jax.shard_map(
        body, mesh=mesh, in_specs=placed, out_specs=P("section", "ctx", None), check_vma=False
    )
```
